256 devices in a mesh: adapter: 32 (over z, x), feature: 8 (over y, core).
Axes of the slice: x: 4, y: 4, z: 8, core: 2. Of those that a mesh axis runs over, the one named last changes fastest.
Arguments:
- adapter_down: bfloat16 [512, 16, 8192], P('adapter', None, 'feature'), may hold values from -6 to 6
- adapter_up: bfloat16 [512, 16, 8192], P('adapter', None, 'feature'), may hold values from -6 to 6
- fisher: float32 [512], P('adapter'), may hold values from 0.1 to 10
- init_v: float32 [8192, 64], P('feature'), may hold values from -0.0625 to 0.0625
- init_u: float32 [8192, 64], P('feature'), may hold values from -0.0625 to 0.0625
- prompt_rows: bfloat16 [16384, 8192], P('adapter', 'feature'), may hold values from -6 to 6
- request_ids: int32 [128], P('adapter'), may hold values from 0 to 511
Outputs:
- served: bfloat16 [16384, 8192], P('adapter', 'feature')
The draws below stay inside these ranges and needn't reach their ends.
All inputs are finite; a program needn't handle non-finite values.
Results may differ from the reference program's by a relative error of at most 0.025.
Values may be sent and summed in bfloat16 or wider, within the bound.
No kernel may reach another device: no remote copies, remote signals or barrier semaphores. Data moves between devices by JAX's collectives and lax.ppermute only.
A program may use at most 64 MiB of HBM per device.

```python
import math
import jax
import jax.numpy as jnp
import numpy as np
from jax import lax

D = 8192
RANK = 16
BASIS = 64
SWEEPS = 3
BLOCK_ROWS = 128
ADAPTERS = 512
ROWS = 16384
BLOCKS = 128


def touch_ends(drawn, stream_key, low, top_value):
    longest = drawn.shape.index(max(drawn.shape))
    spots = []
    for shift in (0, 1):
        where = [jax.random.randint(jax.random.fold_in(stream_key, axis), (), 0, length) for axis, length in enumerate(drawn.shape)]
        where[longest] = (where[longest] + shift) % drawn.shape[longest]
        spots.append(tuple(where))
    return drawn.at[spots[0]].set(low).at[spots[1]].set(top_value)


def steps_of(rng, shape, split, smallest, top_value):
    def one(dim, shards_of):
        steps = jax.random.uniform(jax.random.fold_in(jax.random.fold_in(rng, 6), dim), (shards_of,), jnp.float32, smallest / len(split), top_value / len(split))
        return jnp.repeat(jnp.exp(steps), shape[dim] // shards_of).reshape((-1,) + (1,) * (len(shape) - dim - 1))

    level = one(*split[0])
    for cut in split[1:]:
        level = level * one(*cut)
    return level


def rank_bounds(number_of, skew):
    weights = [(1 << 20) // math.isqrt(grade ** skew) + 1 for grade in range(1, number_of + 1)]
    scale = 1 + sum(weights) // (1 << 30)
    return np.cumsum(np.array([max(1, weight // scale) for weight in weights]))


def ranked(stream_key, extent, number_of, slope):
    grid = rank_bounds(number_of, slope)
    lot = jax.random.randint(jax.random.fold_in(stream_key, 1), extent, 0, int(grid[number_of - 1]))
    grade = jnp.searchsorted(jnp.asarray(grid, jnp.int32), lot, side="right")
    return jax.random.permutation(jax.random.fold_in(stream_key, 2), number_of)[grade].astype(jnp.int32)


def gaussian(key, dims, scale, limit, shards=(), dtype=jnp.bfloat16):
    array = scale * jax.random.normal(key, dims, jnp.float32)
    if shards:
        array = array * steps_of(key, dims, shards, -0.22, 0.18)
    return jnp.clip(array, -limit, limit).astype(dtype)


def setup_inputs(seed: int = 0) -> dict:
    key_list = jax.random.split(jax.random.key(seed), 8)
    return {
        "adapter_down": gaussian(key_list[0], (ADAPTERS, RANK, D), 1.0, 6.0, ((0, 32), (2, 8))),
        "adapter_up": gaussian(key_list[1], (ADAPTERS, RANK, D), 1.0, 6.0, ((0, 32), (2, 8))),
        "fisher": jnp.clip(jnp.exp(math.log(10.0) - 4.6051702 * jax.random.uniform(key_list[2], (ADAPTERS,), jnp.float32) ** steps_of(key_list[2], (ADAPTERS,), ((0, 32),), -0.2, 0.2)), 0.1, 10.0),
        "init_v": gaussian(key_list[3], (D, BASIS), D ** -0.5, 0.0625, ((0, 8),), jnp.float32),
        "init_u": gaussian(key_list[4], (D, BASIS), D ** -0.5, 0.0625, ((0, 8),), jnp.float32),
        "prompt_rows": gaussian(key_list[5], (ROWS, D), 1.0, 6.0, ((0, 32), (1, 8))),
        "request_ids": touch_ends(ranked(key_list[6], (BLOCKS,), ADAPTERS, 2), jax.random.fold_in(key_list[6], 3), 0, ADAPTERS - 1).astype(jnp.int32),
    }


highest = lax.Precision.HIGHEST

def project(adapter_stack, basis_low):
    flat = adapter_stack.reshape(-1, adapter_stack.shape[-1])
    result = jnp.dot(flat.astype(jnp.float32), basis_low.astype(jnp.float32), preferred_element_type=jnp.float32)
    return result.reshape(adapter_stack.shape[0], adapter_stack.shape[1], -1)

def core_of(cols_q, rows_p):
    return jnp.einsum('irk,irl->ikl', cols_q, rows_p, precision=highest)

def numerator(adapter_stack, weighted):
    flat = adapter_stack.reshape(-1, adapter_stack.shape[-1])
    terms = weighted.reshape(-1, weighted.shape[-1])
    return lax.dot_general(flat.astype(jnp.float32), terms.astype(jnp.float32), (((0,), (0,)), ((), ())), preferred_element_type=jnp.float32)

def orthonormal(matrix):
    gram_sum = jnp.dot(matrix.T, matrix, precision=highest)
    factor = jnp.linalg.cholesky(gram_sum)
    return lax.linalg.triangular_solve(factor, matrix, left_side=False, lower=True, transpose_a=True)

def reference(adapter_down, adapter_up, fisher, init_v, init_u, prompt_rows, request_ids):
    basis_v = init_v
    basis_u = init_u
    weights = fisher[:, None, None]
    cols_q = project(adapter_up, basis_u.astype(jnp.bfloat16))
    for sweep_index in range(SWEEPS):
        rows_p = project(adapter_down, basis_v.astype(jnp.bfloat16))
        core_stack = core_of(cols_q, rows_p)
        weighted = (weights * jnp.einsum('irl,ikl->irk', rows_p, core_stack, precision=highest)).astype(jnp.bfloat16)
        basis_u = orthonormal(numerator(adapter_up, weighted))
        cols_q = project(adapter_up, basis_u.astype(jnp.bfloat16))
        core_stack = core_of(cols_q, rows_p)
        weighted = (weights * jnp.einsum('irk,ikl->irl', cols_q, core_stack, precision=highest)).astype(jnp.bfloat16)
        basis_v = orthonormal(numerator(adapter_down, weighted))
    rows_p = project(adapter_down, basis_v.astype(jnp.bfloat16))
    final_cores = core_of(cols_q, rows_p).astype(jnp.bfloat16)
    hidden = jnp.dot(prompt_rows.astype(jnp.float32), basis_v.astype(jnp.bfloat16).astype(jnp.float32), preferred_element_type=jnp.float32).astype(jnp.bfloat16)
    chosen = final_cores[request_ids.astype(jnp.int32)]
    blocked = hidden.reshape(BLOCKS, BLOCK_ROWS, BASIS)
    mixed_rows = jnp.einsum('bnl,bkl->bnk', blocked.astype(jnp.float32), chosen.astype(jnp.float32)).astype(jnp.bfloat16)
    served = jnp.dot(mixed_rows.reshape(ROWS, BASIS).astype(jnp.float32), basis_u.astype(jnp.bfloat16).T.astype(jnp.float32), preferred_element_type=jnp.float32)
    return served.astype(jnp.bfloat16)
```

```python
import jax
import jax.numpy as jnp
from jax import lax
from jax.experimental import pallas as pl
from jax.experimental.pallas import tpu as pltpu
from jax.sharding import PartitionSpec as P

SWEEPS = 3
RANK = 16
BF = jnp.bfloat16
F32 = jnp.float32
highest = lax.Precision.HIGHEST


def call(body, outs, *args):
    whole = pl.BlockSpec(memory_space=pltpu.VMEM)
    single = not isinstance(outs, (list, tuple))
    return pl.pallas_call(
        body,
        out_shape=outs,
        in_specs=[whole] * len(args),
        out_specs=whole if single else [whole] * len(outs),
        compiler_params=pltpu.CompilerParams(vmem_limit_bytes=40 * 1024 * 1024),
    )(*args)


def shape(dims, dtype):
    return jax.ShapeDtypeStruct(dims, dtype)


def dot_nt(a, b, precision=None):
    return lax.dot_general(
        a, b, (((1,), (1,)), ((), ())), preferred_element_type=F32, precision=precision
    )


def dot_tn(a, b, precision=None):
    return lax.dot_general(
        a, b, (((0,), (0,)), ((), ())), preferred_element_type=F32, precision=precision
    )


def dot_nn(a, b, precision=None):
    return jnp.dot(a, b, preferred_element_type=F32, precision=precision)


def inverse_factor(gram):
    size = gram.shape[0]
    rows = lax.broadcasted_iota(jnp.int32, (size, size), 0)
    lanes = lax.broadcasted_iota(jnp.int32, (size, size), 1)
    work = jnp.concatenate([gram, (rows == lanes).astype(F32)], axis=1)
    row_of = lax.broadcasted_iota(jnp.int32, work.shape, 0)
    for k in range(size - 1):
        row = work[k : k + 1, :]
        scaled = row / work[k : k + 1, k : k + 1]
        column = jnp.where(row_of > k, jnp.broadcast_to(work[:, k : k + 1], work.shape), 0.0)
        work = work - column * scaled
    diagonal = jnp.sum(jnp.where(rows == lanes, work[:, :size], 0.0), axis=1, keepdims=True)
    return work[:, size:] * lax.rsqrt(diagonal)


def write_copies(ref, value):
    for i in range(ref.shape[0]):
        ref[i] = value


def summed(ref):
    total = ref[0].astype(F32)
    for i in range(1, ref.shape[0]):
        total = total + ref[i].astype(F32)
    return total


def write_tiles(ref, value):
    across = value.shape[1] // 128
    for i in range(ref.shape[0]):
        r, c = divmod(i, across)
        ref[i] = value[16 * r : 16 * r + 16, 128 * c : 128 * c + 128].astype(BF)


def read_tiles(ref, width):
    across = width // 128
    down = ref.shape[0] // across
    return jnp.concatenate(
        [
            jnp.concatenate([ref[r * across + c] for c in range(across)], axis=1)
            for r in range(down)
        ],
        axis=0,
    )


def halves(gram):
    high = gram.astype(BF)
    low = (gram - high.astype(F32)).astype(BF)
    return jnp.concatenate([high, low], axis=1)


def weighted_terms(fresh, other, fisher_row):
    count = fresh.shape[1]
    inner = dot_tn(fresh, fresh, highest)
    a = lax.broadcasted_iota(jnp.int32, (count, count), 0) // RANK
    b = lax.broadcasted_iota(jnp.int32, (count, count), 1) // RANK
    inner = jnp.where(a == b, inner, 0.0)
    return (dot_nn(other, inner, highest) * fisher_row).astype(BF)


def start_body(down, up, vt, ut, out):
    q = dot_nt(ut[...], up[...]).astype(BF)
    p = dot_nt(vt[...], down[...]).astype(BF)
    write_copies(out, jnp.concatenate([q, p], axis=1))


def first_body(parts, stack, fisher_row, tiles, q_out, p_out):
    total = summed(parts)
    count = total.shape[1] // 2
    q, p = total[:, :count], total[:, count:]
    q_out[...] = q
    p_out[...] = p
    terms = weighted_terms(p, q, fisher_row[...])
    write_tiles(tiles, dot_nn(terms, stack[...]))


def sum_body(parts, out):
    write_copies(out, summed(parts).astype(BF))


def project_body(tiles, stack, out):
    numer = read_tiles(tiles, stack.shape[1])
    y = dot_nt(numer, stack[...]).astype(BF)
    gram = dot_nt(numer, numer)
    write_copies(out, jnp.concatenate([y, halves(gram)], axis=1))


def split_gram(total, at, size):
    return total[:, at : at + size] + total[:, at + size : at + 2 * size]


def renew_body(parts, other, stack, fisher_row, tiles, fresh_out):
    total = summed(parts)
    size, count = other.shape
    inverse = inverse_factor(split_gram(total, count, size))
    fresh = dot_nn(inverse, total[:, :count], highest)
    fresh_out[...] = fresh
    terms = weighted_terms(fresh, other[...], fisher_row[...])
    write_tiles(tiles, dot_nn(terms, stack[...]))


def last_renew_body(parts, other, stack, fisher_row, numer_tiles, tiles, fresh_out, basis_out):
    total = summed(parts)
    size, count = other.shape
    inverse = inverse_factor(split_gram(total, count, size))
    fresh = dot_nn(inverse, total[:, :count], highest)
    fresh_out[...] = fresh
    terms = weighted_terms(fresh, other[...], fisher_row[...])
    write_tiles(tiles, dot_nn(terms, stack[...]))
    numer = read_tiles(numer_tiles, stack.shape[1]).astype(F32)
    basis_out[...] = dot_nn(inverse, numer, highest).astype(BF)


def pick_body(tiles, stack, prompts, q_ref, ids, picked, rest):
    numer = read_tiles(tiles, stack.shape[1])
    z = dot_nt(stack[...], numer).astype(BF)
    q = q_ref[...].T.astype(BF)
    both = jnp.concatenate([z, q], axis=1)
    count = both.shape[0]
    wanted = picked.shape[0] * picked.shape[1]
    r = lax.broadcasted_iota(jnp.int32, (wanted, count), 0)
    c = lax.broadcasted_iota(jnp.int32, (wanted, count), 1)
    hot = ids[...] * RANK + (r & (RANK - 1)) == c
    chosen = dot_nn(hot.astype(F32).astype(BF), both).astype(BF)
    each = picked.shape[1]
    for i in range(picked.shape[0]):
        picked[i] = chosen[i * each : (i + 1) * each]
    hidden = dot_nt(numer, prompts[...]).astype(BF)
    rest[...] = jnp.concatenate([hidden, halves(dot_nt(numer, numer))], axis=1)


def join_body(parts, rest, out, own):
    total = summed(parts).astype(BF)
    own[...] = total
    write_copies(out, jnp.concatenate([rest[...], total], axis=1))


def serve_body(parts, own, basis, out):
    total = summed(parts)
    size = total.shape[0]
    rows = out.shape[0]
    inverse = inverse_factor(split_gram(total, rows, size))
    hidden = dot_nn(inverse, total[:, :rows], highest).astype(BF)
    z = total[:, rows + 2 * size : rows + 3 * size]
    p = dot_nt(z, inverse, highest)
    q = own[...][:, size:].astype(F32)
    blocks = own.shape[0] // RANK
    each = rows // blocks
    for j in range(blocks):
        take = slice(j * RANK, (j + 1) * RANK)
        core = dot_tn(q[take], p[take], highest).astype(BF)
        mixed = dot_nn(core, hidden[:, j * each : (j + 1) * each]).astype(BF)
        out[j * each : (j + 1) * each, :] = dot_tn(mixed, basis[...]).astype(BF)


def swap(parts, axis):
    return lax.all_to_all(parts, axis, 0, 0, tiled=True)


def on_device(adapter_down, adapter_up, fisher, init_v, init_u, prompt_rows, request_ids):
    ways = lax.axis_size("adapter")
    shares = lax.axis_size("feature")
    width = adapter_down.shape[-1]
    size = init_v.shape[1]
    down = adapter_down.reshape(-1, width)
    up = adapter_up.reshape(-1, width)
    count = down.shape[0]
    rows = prompt_rows.shape[0]
    fisher_row = jnp.repeat(fisher, RANK)[None, :]
    tile_shape = shape((ways, size * width // ways // 128, 128), BF)
    flat = shape((size, count), F32)

    every_id = lax.all_to_all(
        jnp.broadcast_to(request_ids[None], (ways, *request_ids.shape)), "adapter", 0, 0, tiled=True
    ).reshape(-1)
    local_id = every_id - lax.axis_index("adapter") * fisher.shape[0]
    pick_rows = jnp.repeat(local_id, RANK)[:, None]

    def reduced(tiles):
        parts = swap(tiles, "adapter")
        return swap(call(sum_body, tile_shape, parts), "adapter")

    def projected(numer, stack):
        parts = call(project_body, shape((shares, size, count + 2 * size), BF), numer, stack)
        return swap(parts, "feature")

    parts = call(
        start_body,
        shape((shares, size, 2 * count), BF),
        down,
        up,
        init_v.T.astype(BF),
        init_u.T.astype(BF),
    )
    tiles, q, p = call(
        first_body, [tile_shape, flat, flat], swap(parts, "feature"), up, fisher_row
    )
    for sweep in range(SWEEPS):
        numer = reduced(tiles)
        parts = projected(numer, up)
        if sweep < SWEEPS - 1:
            tiles, q = call(renew_body, [tile_shape, flat], parts, p, down, fisher_row)
            parts = projected(reduced(tiles), down)
            tiles, p = call(renew_body, [tile_shape, flat], parts, q, up, fisher_row)
        else:
            tiles, q, basis = call(
                last_renew_body,
                [tile_shape, flat, shape((size, width), BF)],
                parts,
                p,
                down,
                fisher_row,
                numer,
            )
    numer = reduced(tiles)
    asked = request_ids.shape[0] * RANK
    picked, rest = call(
        pick_body,
        [shape((ways, asked, 2 * size), BF), shape((size, rows + 2 * size), BF)],
        numer,
        down,
        prompt_rows,
        q,
        pick_rows,
    )
    parts, own = call(
        join_body,
        [shape((shares, size, rows + 4 * size), BF), shape((asked, 2 * size), BF)],
        swap(picked, "adapter"),
        rest,
    )
    return call(
        serve_body, shape((rows, width), BF), swap(parts, "feature"), own, basis
    )


def solution(mesh):
    placed = (
        P("adapter", None, "feature"),
        P("adapter", None, "feature"),
        P("adapter"),
        P("feature", None),
        P("feature", None),
        P("adapter", "feature"),
        P("adapter"),
    )
    return jax.shard_map(
        on_device, mesh=mesh, in_specs=placed, out_specs=P("adapter", "feature"), check_vma=False
    )
```

```python
import jax
import jax.numpy as jnp
from jax import lax
from jax.experimental import pallas as pl
from jax.experimental.pallas import tpu as pltpu
from jax.sharding import PartitionSpec as P

SWEEPS = 3
RANK = 16
XS, YS, CORES = 4, 4, 2
BF = jnp.bfloat16
F32 = jnp.float32
highest = lax.Precision.HIGHEST


def call(body, outs, scratch, *args):
    whole = pl.BlockSpec(memory_space=pltpu.VMEM)
    scalar = pl.BlockSpec(memory_space=pltpu.SMEM)
    single = not isinstance(outs, (list, tuple))
    return pl.pallas_call(
        body,
        out_shape=outs,
        in_specs=[scalar if arg.shape == (1,) else whole for arg in args],
        out_specs=whole if single else [whole] * len(outs),
        scratch_shapes=scratch,
        compiler_params=pltpu.CompilerParams(vmem_limit_bytes=40 * 1024 * 1024),
    )(*args)


def shape(dims, dtype):
    return jax.ShapeDtypeStruct(dims, dtype)


def dot_nt(a, b, precision=None):
    return lax.dot_general(
        a, b, (((1,), (1,)), ((), ())), preferred_element_type=F32, precision=precision
    )


def dot_tn(a, b, precision=None):
    return lax.dot_general(
        a, b, (((0,), (0,)), ((), ())), preferred_element_type=F32, precision=precision
    )


def dot_nn(a, b, precision=None):
    return jnp.dot(a, b, preferred_element_type=F32, precision=precision)


def inverse_factor(gram):
    size = gram.shape[0]
    rows = lax.broadcasted_iota(jnp.int32, (size, size), 0)
    lanes = lax.broadcasted_iota(jnp.int32, (size, size), 1)
    work = jnp.concatenate([gram, (rows == lanes).astype(F32)], axis=1)
    row_of = lax.broadcasted_iota(jnp.int32, work.shape, 0)
    for k in range(size - 1):
        row = work[k : k + 1, :]
        scaled = row / work[k : k + 1, k : k + 1]
        column = jnp.where(row_of > k, jnp.broadcast_to(work[:, k : k + 1], work.shape), 0.0)
        work = work - column * scaled
    diagonal = jnp.sum(jnp.where(rows == lanes, work[:, :size], 0.0), axis=1, keepdims=True)
    return work[:, size:] * lax.rsqrt(diagonal)


def write_copies(ref, value):
    for i in range(ref.shape[0]):
        ref[i] = value


def halves(gram):
    high = gram.astype(BF)
    low = (gram - high.astype(F32)).astype(BF)
    return jnp.concatenate([high, low], axis=1)


def weighted_terms(fresh, other, fisher_row):
    count = fresh.shape[1]
    inner = dot_tn(fresh, fresh, highest)
    a = lax.broadcasted_iota(jnp.int32, (count, count), 0) // RANK
    b = lax.broadcasted_iota(jnp.int32, (count, count), 1) // RANK
    inner = jnp.where(a == b, inner, 0.0)
    return (dot_nn(other, inner, highest) * fisher_row).astype(BF)


def added(refs):
    total = refs[0][...].astype(F32)
    for ref in refs[1:]:
        total = total + ref[...].astype(F32)
    return total


def place_quarters(at, terms, stack, hold, quarters):
    each = hold.shape[1]
    for i in range(XS):
        hold[i] = dot_nn(terms[i * each : (i + 1) * each], stack[...]).astype(BF)
    for d, ref in enumerate(quarters):
        ref[...] = hold[lax.rem(at[0] + d, XS)]


def take_quarters(at, quarters, hold, width):
    for d, ref in enumerate(quarters):
        hold[lax.rem(at[0] + XS - d, XS)] = ref[:, :width]
    return hold[...].reshape(-1, width)


def start_body(down, up, vt, ut, out):
    q = dot_nt(ut[...], up[...])
    p = dot_nt(vt[...], down[...])
    out[...] = jnp.concatenate([q, p], axis=1)


def pair_body(own, got, out):
    total = own[...] + got[...]
    plain = 2 * total.shape[1] - out.shape[1]
    if plain == total.shape[1]:
        out[...] = total.astype(BF)
    else:
        out[...] = jnp.concatenate([total[:, :plain].astype(BF), halves(total[:, plain:])], axis=1)


def first_body(at, a, b, c, d, stack, fisher_row, k0, k1, k2, k3, q_out, p_out, hold):
    total = added((a, b, c, d))
    count = total.shape[1] // 2
    q, p = total[:, :count], total[:, count:]
    q_out[...] = q
    p_out[...] = p
    terms = weighted_terms(p, q, fisher_row[...])
    place_quarters(at, terms, stack, hold, (k0, k1, k2, k3))


def gather_x_body(a, b, c, d, out):
    write_copies(out, added((a, b, c, d)).astype(BF))


def gather_x_ids_body(a, b, c, d, ids, out):
    write_copies(out, jnp.concatenate([added((a, b, c, d)).astype(BF), ids[...]], axis=1))


def sum_body(parts, out):
    total = parts[0].astype(F32)
    for i in range(1, parts.shape[0]):
        total = total + parts[i].astype(F32)
    out[...] = total.astype(BF)


def project_body(at, a, b, c, d, stack, out, numer_out, hold):
    numer = take_quarters(at, (a, b, c, d), hold, stack.shape[1])
    numer_out[...] = numer
    out[...] = jnp.concatenate([dot_nt(numer, stack[...]), dot_nt(numer, numer)], axis=1)


def project_ids_body(at, a, b, c, d, stack, out, numer_out, ids_out, hold):
    project_body(at, a, b, c, d, stack, out, numer_out, hold)
    ids = added([ref.at[:, stack.shape[1] :] for ref in (a, b, c, d)])
    ids_out[...] = (ids[0:1] * RANK + ids[1:2]).astype(jnp.int32)


def split_gram(total, at, size):
    return total[:, at : at + size] + total[:, at + size : at + 2 * size]


def renew(at, parts, other, stack, fisher_row, quarters, fresh_out, hold):
    total = added(parts)
    size, count = other.shape
    inverse = inverse_factor(split_gram(total, count, size))
    fresh = dot_nn(inverse, total[:, :count], highest)
    fresh_out[...] = fresh
    terms = weighted_terms(fresh, other[...], fisher_row[...])
    place_quarters(at, terms, stack, hold, quarters)
    return inverse


def renew_body(at, a, b, c, d, other, stack, fisher_row, k0, k1, k2, k3, fresh_out, hold):
    renew(at, (a, b, c, d), other, stack, fisher_row, (k0, k1, k2, k3), fresh_out, hold)


def last_renew_body(
    at, a, b, c, d, other, stack, fisher_row, numer, k0, k1, k2, k3, fresh_out, basis_out, hold
):
    inverse = renew(
        at, (a, b, c, d), other, stack, fisher_row, (k0, k1, k2, k3), fresh_out, hold
    )
    basis_out[...] = dot_nn(inverse, numer[...].astype(F32), highest).astype(BF)


def pick_body(at, a, b, c, d, stack, prompts, q_ref, ids, picked, hidden_out, gram_out, hold):
    numer = take_quarters(at, (a, b, c, d), hold, stack.shape[1])
    z = dot_nt(stack[...], numer).astype(BF)
    q = q_ref[...].T.astype(BF)
    both = jnp.concatenate([z, q], axis=1)
    count = both.shape[0]
    wanted = picked.shape[0] * picked.shape[1]
    r = lax.broadcasted_iota(jnp.int32, (wanted, count), 0)
    c = lax.broadcasted_iota(jnp.int32, (wanted, count), 1)
    hot = ids[...] * RANK + (r & (RANK - 1)) == c
    chosen = dot_nn(hot.astype(F32).astype(BF), both).astype(BF)
    each = picked.shape[1]
    for i in range(picked.shape[0]):
        picked[i] = chosen[i * each : (i + 1) * each]
    hidden_out[...] = dot_nt(numer, prompts[...])
    gram_out[...] = dot_nt(numer, numer)


def join_body(parts, hidden, gram, out, own):
    total = parts[0].astype(F32)
    for i in range(1, parts.shape[0]):
        total = total + parts[i].astype(F32)
    own[...] = total
    size = gram.shape[1]
    out[...] = jnp.concatenate([hidden[...], total[:, :size], gram[...]], axis=1)


def serve_body(a, b, c, d, own, basis, out):
    total = added((a, b, c, d))
    size = total.shape[0]
    rows = out.shape[0]
    inverse = inverse_factor(split_gram(total, rows + size, size))
    hidden = dot_nn(inverse, total[:, :rows], highest).astype(BF)
    z = total[:, rows : rows + size]
    p = dot_nt(z, inverse, highest)
    q = own[...][:, size:]
    blocks = own.shape[0] // RANK
    each = rows // blocks
    for j in range(blocks):
        take = slice(j * RANK, (j + 1) * RANK)
        core = dot_tn(q[take], p[take], highest).astype(BF)
        mixed = dot_nn(core, hidden[:, j * each : (j + 1) * each]).astype(BF)
        out[j * each : (j + 1) * each, :] = dot_tn(mixed, basis[...]).astype(BF)


def around_x(value, d):
    size = lax.axis_size("adapter")
    return lax.ppermute(
        value, "adapter", [(i, i // XS * XS + (i + d) % XS) for i in range(size)]
    )


def around_y(value, d):
    size = lax.axis_size("feature")
    return lax.ppermute(value, "feature", [(i, (i + d * CORES) % size) for i in range(size)])


def other_core(value):
    size = lax.axis_size("feature")
    return lax.ppermute(value, "feature", [(i, i ^ 1) for i in range(size)])


def over_feature(value, gram_size):
    rows, lanes = value.shape
    pair = call(pair_body, shape((rows, lanes + gram_size), BF), [], value, other_core(value))
    return [pair] + [around_y(pair, d) for d in range(1, YS)]


def on_device(adapter_down, adapter_up, fisher, init_v, init_u, prompt_rows, request_ids):
    ways = lax.axis_size("adapter")
    width = adapter_down.shape[-1]
    size = init_v.shape[1]
    down = adapter_down.reshape(-1, width)
    up = adapter_up.reshape(-1, width)
    count = down.shape[0]
    rows = prompt_rows.shape[0]
    blocks = request_ids.shape[0]
    position = lax.axis_index("adapter")
    at = jnp.full((1,), position % XS, jnp.int32)
    fisher_row = jnp.repeat(fisher, RANK)[None, :]
    quarter = size // XS
    hold = [pltpu.VMEM((XS, quarter, width), BF)]
    part = shape((quarter, width), BF)
    flat = shape((size, count), F32)
    digits = jnp.stack([request_ids // RANK, request_ids % RANK]).astype(BF)
    id_tile = lax.dynamic_update_slice(
        jnp.zeros((quarter, ways * blocks), BF), digits, (0, position * blocks)
    )
    z_groups = [[z * XS + x for z in range(ways // XS)] for x in range(XS)]

    def summed_quarters(quarters, ids=None):
        came = [quarters[0]] + [around_x(quarters[d], d) for d in range(1, XS)]
        if ids is None:
            lanes = width
            copies = call(
                gather_x_body, shape((ways // XS, quarter, lanes), BF), [], *came
            )
        else:
            lanes = width + ids.shape[1]
            copies = call(
                gather_x_ids_body, shape((ways // XS, quarter, lanes), BF), [], *came, ids
            )
        parts = lax.all_to_all(
            copies, "adapter", 0, 0, axis_index_groups=z_groups, tiled=True
        )
        own = call(sum_body, shape((quarter, lanes), BF), [], parts)
        return [own] + [around_x(own, d) for d in range(1, XS)]

    def projected(quarters, stack):
        outs = [shape((size, count + size), F32), shape((size, width), BF)]
        value, numer = call(project_body, outs, hold, at, *quarters, stack)
        return over_feature(value, size), numer

    value = call(
        start_body,
        shape((size, 2 * count), F32),
        [],
        down,
        up,
        init_v.T.astype(BF),
        init_u.T.astype(BF),
    )
    *quarters, q, p = call(
        first_body, [part] * XS + [flat, flat], hold, at, *over_feature(value, 0), up, fisher_row
    )
    for sweep in range(SWEEPS):
        if sweep == 0:
            value, _, every_id = call(
                project_ids_body,
                [
                    shape((size, count + size), F32),
                    shape((size, width), BF),
                    shape((1, ways * blocks), jnp.int32),
                ],
                hold,
                at,
                *summed_quarters(quarters, id_tile),
                up,
            )
            parts = over_feature(value, size)
        else:
            parts, numer = projected(summed_quarters(quarters), up)
        if sweep < SWEEPS - 1:
            *quarters, q = call(
                renew_body, [part] * XS + [flat], hold, at, *parts, p, down, fisher_row
            )
            parts, _ = projected(summed_quarters(quarters), down)
            *quarters, p = call(
                renew_body, [part] * XS + [flat], hold, at, *parts, q, up, fisher_row
            )
        else:
            *quarters, q, basis = call(
                last_renew_body,
                [part] * XS + [flat, shape((size, width), BF)],
                hold,
                at,
                *parts,
                p,
                down,
                fisher_row,
                numer,
            )
    pick_rows = jnp.repeat(every_id[0] - position * fisher.shape[0], RANK)[:, None]
    asked = blocks * RANK
    picked, hidden, gram = call(
        pick_body,
        [shape((ways, asked, 2 * size), BF), shape((size, rows), F32), shape((size, size), F32)],
        hold,
        at,
        *summed_quarters(quarters),
        down,
        prompt_rows,
        q,
        pick_rows,
    )
    value, own = call(
        join_body,
        [shape((size, rows + 2 * size), F32), shape((asked, 2 * size), F32)],
        [],
        lax.all_to_all(picked, "adapter", 0, 0, tiled=True),
        hidden,
        gram,
    )
    return call(
        serve_body, shape((rows, width), BF), [], *over_feature(value, size), own, basis
    )


def solution(mesh):
    placed = (
        P("adapter", None, "feature"),
        P("adapter", None, "feature"),
        P("adapter"),
        P("feature", None),
        P("feature", None),
        P("adapter", "feature"),
        P("adapter"),
    )
    return jax.shard_map(
        on_device, mesh=mesh, in_specs=placed, out_specs=P("adapter", "feature"), check_vma=False
    )
```

```python
import jax
import jax.numpy as jnp
from jax import lax
from jax.experimental import pallas as pl
from jax.experimental.pallas import tpu as pltpu
from jax.sharding import PartitionSpec as P

SWEEPS = 3
RANK = 16
CORES = 2
BF = jnp.bfloat16
F32 = jnp.float32
highest = lax.Precision.HIGHEST


def call(body, outs, *args):
    whole = pl.BlockSpec(memory_space=pltpu.VMEM)
    single = not isinstance(outs, (list, tuple))
    return pl.pallas_call(
        body,
        out_shape=outs,
        in_specs=[whole] * len(args),
        out_specs=whole if single else [whole] * len(outs),
        compiler_params=pltpu.CompilerParams(vmem_limit_bytes=40 * 1024 * 1024),
    )(*args)


def shape(dims, dtype):
    return jax.ShapeDtypeStruct(dims, dtype)


def dot_nt(a, b, precision=None):
    return lax.dot_general(
        a, b, (((1,), (1,)), ((), ())), preferred_element_type=F32, precision=precision
    )


def dot_tn(a, b, precision=None):
    return lax.dot_general(
        a, b, (((0,), (0,)), ((), ())), preferred_element_type=F32, precision=precision
    )


def dot_nn(a, b, precision=None):
    return jnp.dot(a, b, preferred_element_type=F32, precision=precision)


def inverse_factor(gram):
    size = gram.shape[0]
    rows = lax.broadcasted_iota(jnp.int32, (size, size), 0)
    lanes = lax.broadcasted_iota(jnp.int32, (size, size), 1)
    eye = rows == lanes
    diagonal = jnp.where(eye, gram, 0.0)
    by_row = lax.rsqrt(jnp.sum(diagonal, axis=1, keepdims=True))
    by_lane = lax.rsqrt(jnp.sum(diagonal, axis=0, keepdims=True))
    work = jnp.concatenate([gram * by_row * by_lane, eye.astype(F32)], axis=1)
    group = 8
    whole = (group, 2 * size)
    blocks = [work[group * i : group * (i + 1)] for i in range(size // group)]
    within = lax.broadcasted_iota(jnp.int32, whole, 0)
    for b in range(len(blocks)):
        first = group * b
        columns = [
            {
                j: jnp.broadcast_to(blocks[j][:, first + m : first + m + 1], whole)
                for j in range(b, len(blocks))
            }
            for m in range(group)
        ]
        pivot_rows = [blocks[b][i : i + 1] for i in range(group)]
        pivots = {
            (i, m): columns[m][b][i : i + 1] for i in range(group) for m in range(i, group)
        }
        solved = []
        for p in range(0, group, 2):
            top, mix, low = pivots[p, p], pivots[p, p + 1], pivots[p + 1, p + 1]
            over = 1.0 / (top * low - mix * mix)
            a, b01, c = low * over, -mix * over, top * over
            factors = []
            for i in range(p + 2, group):
                x, y = pivots[p, i], pivots[p + 1, i]
                factors.append((i, a * x + b01 * y, b01 * x + c * y))
            for i, u, v in factors:
                for m in range(i, group):
                    pivots[i, m] = pivots[i, m] - (u * pivots[p, m] + v * pivots[p + 1, m])
                pivot_rows[i] = pivot_rows[i] - (u * pivot_rows[p] + v * pivot_rows[p + 1])
            solved.append((a, b01, c, factors))
        terms = [None] * group
        for p in range(group - 2, -1, -2):
            a, b01, c, factors = solved[p // 2]
            t0 = a * pivot_rows[p] + b01 * pivot_rows[p + 1]
            t1 = b01 * pivot_rows[p] + c * pivot_rows[p + 1]
            for i, u, v in factors:
                t0 = t0 - u * terms[i]
                t1 = t1 - v * terms[i]
            terms[p], terms[p + 1] = t0, t1
        for j in range(b + 1, len(blocks)):
            for m in range(group):
                blocks[j] = blocks[j] - columns[m][j] * terms[m]
        done = blocks[b]
        for p in range(0, group, 2):
            second = pivot_rows[p + 1] - (pivots[p, p + 1] / pivots[p, p]) * pivot_rows[p]
            done = jnp.where(within == p, pivot_rows[p], done)
            done = jnp.where(within == p + 1, second, done)
        blocks[b] = done
    work = jnp.concatenate(blocks, axis=0)
    diagonal = jnp.sum(jnp.where(eye, work[:, :size], 0.0), axis=1, keepdims=True)
    return work[:, size:] * lax.rsqrt(diagonal) * by_lane


def write_copies(ref, value):
    for i in range(ref.shape[0]):
        ref[i] = value


def halves(gram):
    high = gram.astype(BF)
    low = (gram - high.astype(F32)).astype(BF)
    return jnp.concatenate([high, low], axis=1)


def weighted_terms(fresh, other, fisher_row):
    count = fresh.shape[1]
    inner = dot_tn(fresh, fresh, highest)
    a = lax.broadcasted_iota(jnp.int32, (count, count), 0) // RANK
    b = lax.broadcasted_iota(jnp.int32, (count, count), 1) // RANK
    inner = jnp.where(a == b, inner, 0.0)
    return (dot_nn(other, inner, highest) * fisher_row).astype(BF)


def added(refs):
    total = refs[0][...].astype(F32)
    for ref in refs[1:]:
        total = total + ref[...].astype(F32)
    return total


def write_tiles(ref, value):
    across = value.shape[1] // 128
    for i in range(ref.shape[0]):
        r, c = divmod(i, across)
        ref[i] = value[16 * r : 16 * r + 16, 128 * c : 128 * c + 128].astype(BF)


def read_tiles(ref, width):
    across = width // 128
    down = ref.shape[0] // across
    return jnp.concatenate(
        [
            jnp.concatenate([ref[r * across + c, :16] for c in range(across)], axis=1)
            for r in range(down)
        ],
        axis=0,
    )


def start_body(down, up, vt, ut, out):
    q = dot_nt(ut[...], up[...])
    p = dot_nt(vt[...], down[...])
    out[...] = jnp.concatenate([q, p], axis=1)


def pair_body(own, got, out):
    total = own[...] + got[...]
    plain = 2 * total.shape[1] - out.shape[1]
    if plain == total.shape[1]:
        out[...] = total.astype(BF)
    else:
        out[...] = jnp.concatenate([total[:, :plain].astype(BF), halves(total[:, plain:])], axis=1)


def first_body(a, b, c, d, stack, fisher_row, tiles, q_out, p_out):
    total = added((a, b, c, d))
    count = total.shape[1] // 2
    q, p = total[:, :count], total[:, count:]
    q_out[...] = q
    p_out[...] = p
    terms = weighted_terms(p, q, fisher_row[...])
    write_tiles(tiles, dot_nn(terms, stack[...]))


def summed(ref):
    total = ref[0].astype(F32)
    for i in range(1, ref.shape[0]):
        total = total + ref[i].astype(F32)
    return total


def sum_body(parts, out):
    write_copies(out, summed(parts).astype(BF))


def sum_ids_body(parts, ids, out):
    write_copies(out, jnp.concatenate([summed(parts).astype(BF), ids[...]], axis=0))


def project_body(tiles, stack, out):
    numer = read_tiles(tiles, stack.shape[1])
    out[...] = jnp.concatenate([dot_nt(numer, stack[...]), dot_nt(numer, numer)], axis=1)


def project_ids_body(tiles, stack, out, ids_out):
    project_body(tiles, stack, out)
    ids = summed(tiles.at[:, 16:])
    ids_out[...] = (ids[0:1] * RANK + ids[1:2]).astype(jnp.int32)


def split_gram(total, at, size):
    return total[:, at : at + size] + total[:, at + size : at + 2 * size]


def renew(parts, other, stack, fisher_row, tiles, fresh_out):
    total = added(parts)
    size, count = other.shape
    inverse = inverse_factor(split_gram(total, count, size))
    fresh = dot_nn(inverse, total[:, :count], highest)
    fresh_out[...] = fresh
    terms = weighted_terms(fresh, other[...], fisher_row[...])
    write_tiles(tiles, dot_nn(terms, stack[...]))
    return inverse


def renew_body(a, b, c, d, other, stack, fisher_row, tiles, fresh_out):
    renew((a, b, c, d), other, stack, fisher_row, tiles, fresh_out)


def last_renew_body(
    a, b, c, d, other, stack, fisher_row, numer_tiles, tiles, fresh_out, basis_out
):
    inverse = renew((a, b, c, d), other, stack, fisher_row, tiles, fresh_out)
    numer = read_tiles(numer_tiles, stack.shape[1]).astype(F32)
    basis_out[...] = dot_nn(inverse, numer, highest).astype(BF)


def pick_body(tiles, stack, prompts, q_ref, ids, picked, hidden_out, gram_out):
    numer = read_tiles(tiles, stack.shape[1])
    z = dot_nt(stack[...], numer).astype(BF)
    q = q_ref[...].T.astype(BF)
    both = jnp.concatenate([z, q], axis=1)
    count = both.shape[0]
    wanted = picked.shape[0] * picked.shape[1]
    r = lax.broadcasted_iota(jnp.int32, (wanted, count), 0)
    c = lax.broadcasted_iota(jnp.int32, (wanted, count), 1)
    hot = ids[...] * RANK + (r & (RANK - 1)) == c
    chosen = dot_nn(hot.astype(F32).astype(BF), both).astype(BF)
    each = picked.shape[1]
    for i in range(picked.shape[0]):
        picked[i] = chosen[i * each : (i + 1) * each]
    hidden_out[...] = dot_nt(numer, prompts[...])
    gram_out[...] = dot_nt(numer, numer)


def join_body(parts, hidden, gram, out, own):
    total = summed(parts)
    own[...] = total
    size = gram.shape[1]
    out[...] = jnp.concatenate([hidden[...], total[:, :size], gram[...]], axis=1)


def serve_body(a, b, c, d, own, basis, out):
    total = added((a, b, c, d))
    size = total.shape[0]
    rows = out.shape[0]
    inverse = inverse_factor(split_gram(total, rows + size, size))
    hidden = dot_nn(inverse, total[:, :rows], highest).astype(BF)
    z = total[:, rows : rows + size]
    p = dot_nt(z, inverse, highest)
    q = own[...][:, size:]
    blocks = own.shape[0] // RANK
    each = rows // blocks
    for j in range(blocks):
        take = slice(j * RANK, (j + 1) * RANK)
        core = dot_tn(q[take], p[take], highest).astype(BF)
        mixed = dot_nn(core, hidden[:, j * each : (j + 1) * each]).astype(BF)
        out[j * each : (j + 1) * each, :] = dot_tn(mixed, basis[...]).astype(BF)


def around_y(value, d):
    size = lax.axis_size("feature")
    return lax.ppermute(value, "feature", [(i, (i + d * CORES) % size) for i in range(size)])


def other_core(value):
    size = lax.axis_size("feature")
    return lax.ppermute(value, "feature", [(i, i ^ 1) for i in range(size)])


def over_feature(value, gram_size):
    rows, lanes = value.shape
    pair = call(pair_body, shape((rows, lanes + gram_size), BF), value, other_core(value))
    return [pair] + [around_y(pair, d) for d in (1, 3, 2)]


def on_device(adapter_down, adapter_up, fisher, init_v, init_u, prompt_rows, request_ids):
    ways = lax.axis_size("adapter")
    width = adapter_down.shape[-1]
    size = init_v.shape[1]
    down = adapter_down.reshape(-1, width)
    up = adapter_up.reshape(-1, width)
    count = down.shape[0]
    rows = prompt_rows.shape[0]
    blocks = request_ids.shape[0]
    position = lax.axis_index("adapter")
    fisher_row = jnp.repeat(fisher, RANK)[None, :]
    tile = (size * width // ways // 128, 128)
    tile_shape = shape((ways, *tile), BF)
    flat = shape((size, count), F32)
    digits = jnp.stack([request_ids // RANK, request_ids % RANK]).astype(BF)
    id_tile = lax.dynamic_update_slice(jnp.zeros(tile, BF), digits, (0, position * blocks))

    def swap(parts):
        return lax.all_to_all(parts, "adapter", 0, 0, tiled=True)

    def reduced(tiles):
        return swap(call(sum_body, tile_shape, swap(tiles)))

    def projected(numer, stack):
        value = call(project_body, shape((size, count + size), F32), numer, stack)
        return over_feature(value, size)

    value = call(
        start_body,
        shape((size, 2 * count), F32),
        down,
        up,
        init_v.T.astype(BF),
        init_u.T.astype(BF),
    )
    tiles, q, p = call(
        first_body, [tile_shape, flat, flat], *over_feature(value, 0), up, fisher_row
    )
    for sweep in range(SWEEPS):
        if sweep == 0:
            copies = call(
                sum_ids_body, shape((ways, 2 * tile[0], 128), BF), swap(tiles), id_tile
            )
            value, every_id = call(
                project_ids_body,
                [shape((size, count + size), F32), shape((1, 128), jnp.int32)],
                swap(copies),
                up,
            )
            parts = over_feature(value, size)
        else:
            numer = reduced(tiles)
            parts = projected(numer, up)
        if sweep < SWEEPS - 1:
            tiles, q = call(renew_body, [tile_shape, flat], *parts, p, down, fisher_row)
            parts = projected(reduced(tiles), down)
            tiles, p = call(renew_body, [tile_shape, flat], *parts, q, up, fisher_row)
        else:
            tiles, q, basis = call(
                last_renew_body,
                [tile_shape, flat, shape((size, width), BF)],
                *parts,
                p,
                down,
                fisher_row,
                numer,
            )
    pick_rows = jnp.repeat(every_id[0, : ways * blocks] - position * fisher.shape[0], RANK)[:, None]
    asked = blocks * RANK
    picked, hidden, gram = call(
        pick_body,
        [shape((ways, asked, 2 * size), BF), shape((size, rows), F32), shape((size, size), F32)],
        reduced(tiles),
        down,
        prompt_rows,
        q,
        pick_rows,
    )
    value, own = call(
        join_body,
        [shape((size, rows + 2 * size), F32), shape((asked, 2 * size), F32)],
        swap(picked),
        hidden,
        gram,
    )
    return call(serve_body, shape((rows, width), BF), *over_feature(value, size), own, basis)


def solution(mesh):
    placed = (
        P("adapter", None, "feature"),
        P("adapter", None, "feature"),
        P("adapter"),
        P("feature", None),
        P("feature", None),
        P("adapter", "feature"),
        P("adapter"),
    )
    return jax.shard_map(
        on_device, mesh=mesh, in_specs=placed, out_specs=P("adapter", "feature"), check_vma=False
    )
```

```python
import jax
import jax.numpy as jnp
from jax import lax
from jax.experimental import pallas as pl
from jax.experimental.pallas import tpu as pltpu
from jax.sharding import PartitionSpec as P

SWEEPS = 3
RANK = 16
CORES = 2
BF = jnp.bfloat16
F32 = jnp.float32


def call(body, outs, *args):
    whole = pl.BlockSpec(memory_space=pltpu.VMEM)
    scalar = pl.BlockSpec(memory_space=pltpu.SMEM)
    single = not isinstance(outs, (list, tuple))
    return pl.pallas_call(
        body,
        out_shape=outs,
        in_specs=[scalar if arg.shape == (1,) else whole for arg in args],
        out_specs=whole if single else [whole] * len(outs),
        compiler_params=pltpu.CompilerParams(vmem_limit_bytes=40 * 1024 * 1024),
    )(*args)


def shape(dims, dtype):
    return jax.ShapeDtypeStruct(dims, dtype)


def dot_nt(a, b, precision=None):
    return lax.dot_general(
        a, b, (((1,), (1,)), ((), ())), preferred_element_type=F32, precision=precision
    )


def dot_tn(a, b, precision=None):
    return lax.dot_general(
        a, b, (((0,), (0,)), ((), ())), preferred_element_type=F32, precision=precision
    )


def dot_nn(a, b, precision=None):
    return jnp.dot(a, b, preferred_element_type=F32, precision=precision)


def in_three(product, a, b):
    a_high, b_high = a.astype(BF), b.astype(BF)
    a_low = (a - a_high.astype(F32)).astype(BF)
    b_low = (b - b_high.astype(F32)).astype(BF)
    return product(a_high, b_high) + (product(a_high, b_low) + product(a_low, b_high))


def inverse_factor(gram):
    size = gram.shape[0]
    rows = lax.broadcasted_iota(jnp.int32, (size, size), 0)
    lanes = lax.broadcasted_iota(jnp.int32, (size, size), 1)
    eye = rows == lanes
    diagonal = jnp.where(eye, gram, 0.0)
    by_row = lax.rsqrt(jnp.sum(diagonal, axis=1, keepdims=True))
    by_lane = lax.rsqrt(jnp.sum(diagonal, axis=0, keepdims=True))
    work = jnp.concatenate([gram * by_row * by_lane, eye.astype(F32)], axis=1)
    group = 8
    whole = (group, 2 * size)
    blocks = [work[group * i : group * (i + 1)] for i in range(size // group)]
    within = lax.broadcasted_iota(jnp.int32, whole, 0)
    for b in range(len(blocks)):
        first = group * b
        columns = [
            {
                j: jnp.broadcast_to(blocks[j][:, first + m : first + m + 1], whole)
                for j in range(b, len(blocks))
            }
            for m in range(group)
        ]
        pivot_rows = [blocks[b][i : i + 1] for i in range(group)]
        pivots = {
            (i, m): columns[m][b][i : i + 1] for i in range(group) for m in range(i, group)
        }
        solved = []
        for p in range(0, group, 2):
            top, mix, low = pivots[p, p], pivots[p, p + 1], pivots[p + 1, p + 1]
            over = 1.0 / (top * low - mix * mix)
            a, b01, c = low * over, -mix * over, top * over
            factors = []
            for i in range(p + 2, group):
                x, y = pivots[p, i], pivots[p + 1, i]
                factors.append((i, a * x + b01 * y, b01 * x + c * y))
            for i, u, v in factors:
                for m in range(i, group):
                    pivots[i, m] = pivots[i, m] - (u * pivots[p, m] + v * pivots[p + 1, m])
                pivot_rows[i] = pivot_rows[i] - (u * pivot_rows[p] + v * pivot_rows[p + 1])
            solved.append((a, b01, c, factors))
        terms = [None] * group
        for p in range(group - 2, -1, -2):
            a, b01, c, factors = solved[p // 2]
            t0 = a * pivot_rows[p] + b01 * pivot_rows[p + 1]
            t1 = b01 * pivot_rows[p] + c * pivot_rows[p + 1]
            for i, u, v in factors:
                t0 = t0 - u * terms[i]
                t1 = t1 - v * terms[i]
            terms[p], terms[p + 1] = t0, t1
        for j in range(b + 1, len(blocks)):
            for m in range(group):
                blocks[j] = blocks[j] - columns[m][j] * terms[m]
        done = blocks[b]
        for p in range(0, group, 2):
            second = pivot_rows[p + 1] - (pivots[p, p + 1] / pivots[p, p]) * pivot_rows[p]
            done = jnp.where(within == p, pivot_rows[p], done)
            done = jnp.where(within == p + 1, second, done)
        blocks[b] = done
    work = jnp.concatenate(blocks, axis=0)
    diagonal = jnp.sum(jnp.where(eye, work[:, :size], 0.0), axis=1, keepdims=True)
    return work[:, size:] * lax.rsqrt(diagonal) * by_lane


def write_copies(ref, value):
    for i in range(ref.shape[0]):
        ref[i] = value


def halves(gram):
    high = gram.astype(BF)
    low = (gram - high.astype(F32)).astype(BF)
    return jnp.concatenate([high, low], axis=1)


def weighted_terms(fresh, other, fisher_row):
    count = fresh.shape[1]
    inner = in_three(dot_tn, fresh, fresh)
    a = lax.broadcasted_iota(jnp.int32, (count, count), 0) // RANK
    b = lax.broadcasted_iota(jnp.int32, (count, count), 1) // RANK
    inner = jnp.where(a == b, inner, 0.0)
    return (in_three(dot_nn, other, inner) * fisher_row).astype(BF)


def added(refs):
    total = refs[0][...].astype(F32)
    for ref in refs[1:]:
        total = total + ref[...].astype(F32)
    return total


def write_tiles(ref, value):
    across = value.shape[1] // 128
    for i in range(ref.shape[0]):
        r, c = divmod(i, across)
        ref[i] = value[16 * r : 16 * r + 16, 128 * c : 128 * c + 128].astype(BF)


def read_tiles(ref, width):
    across = width // 128
    down = ref.shape[0] // across
    return jnp.concatenate(
        [
            jnp.concatenate([ref[r * across + c, :16] for c in range(across)], axis=1)
            for r in range(down)
        ],
        axis=0,
    )


def start_body(down, up, vt, ut, out):
    q = dot_nt(ut[...], up[...])
    p = dot_nt(vt[...], down[...])
    out[...] = jnp.concatenate([q, p], axis=1)


def pair_body(own, got, out):
    total = own[...] + got[...]
    plain = 2 * total.shape[1] - out.shape[1]
    if plain == total.shape[1]:
        out[...] = total.astype(BF)
    else:
        out[...] = jnp.concatenate([total[:, :plain].astype(BF), halves(total[:, plain:])], axis=1)


def first_body(a, b, c, d, stack, fisher_row, tiles, q_out, p_out):
    total = added((a, b, c, d))
    count = total.shape[1] // 2
    q, p = total[:, :count], total[:, count:]
    q_out[...] = q
    p_out[...] = p
    terms = weighted_terms(p, q, fisher_row[...])
    write_tiles(tiles, dot_nn(terms, stack[...]))


def summed(ref):
    total = ref[0].astype(F32)
    for i in range(1, ref.shape[0]):
        total = total + ref[i].astype(F32)
    return total


def sum_body(parts, out):
    write_copies(out, summed(parts).astype(BF))


def sum_ids_body(parts, ids, out):
    write_copies(out, jnp.concatenate([summed(parts).astype(BF), ids[...]], axis=0))


def project_body(tiles, stack, out):
    numer = read_tiles(tiles, stack.shape[1])
    out[...] = jnp.concatenate([dot_nt(numer, stack[...]), dot_nt(numer, numer)], axis=1)


def project_ids_body(tiles, stack, out, ids_out):
    project_body(tiles, stack, out)
    ids = summed(tiles.at[:, 16:])
    ids_out[...] = (ids[0:1] * RANK + ids[1:2]).astype(jnp.int32)


def split_gram(total, at, size):
    return total[:, at : at + size] + total[:, at + size : at + 2 * size]


def renew(parts, other, stack, fisher_row, tiles, fresh_out):
    total = added(parts)
    size, count = other.shape
    inverse = inverse_factor(split_gram(total, count, size))
    fresh = in_three(dot_nn, inverse, total[:, :count])
    fresh_out[...] = fresh
    terms = weighted_terms(fresh, other[...], fisher_row[...])
    write_tiles(tiles, dot_nn(terms, stack[...]))
    return inverse


def renew_body(a, b, c, d, other, stack, fisher_row, tiles, fresh_out):
    renew((a, b, c, d), other, stack, fisher_row, tiles, fresh_out)


def last_renew_body(
    a, b, c, d, other, stack, fisher_row, numer_tiles, tiles, fresh_out, basis_out
):
    inverse = renew((a, b, c, d), other, stack, fisher_row, tiles, fresh_out)
    numer = read_tiles(numer_tiles, stack.shape[1]).astype(F32)
    basis_out[...] = in_three(dot_nn, inverse, numer).astype(BF)


def side_by_side(value):
    half = value.shape[0] // 2
    lanes = lax.broadcasted_iota(jnp.int32, (half, value.shape[1]), 1)
    return jnp.where(lanes < value.shape[1] // 2, value[:half], value[half:])


def one_below_other(value):
    half = value.shape[1] // 2
    return jnp.concatenate([value[:, :half], value[:, half:]], axis=0)


def pick_body(core, tiles, stack, prompts, q_ref, ids, picked, hidden_out, gram_out):
    numer = read_tiles(tiles, stack.shape[1])
    z = dot_nt(stack[...], numer).astype(BF)
    q = q_ref[...].T.astype(BF)
    count, size = z.shape
    ways = picked.shape[0]
    wanted = ids.shape[0]
    r = lax.broadcasted_iota(jnp.int32, (wanted, count), 0)
    c = lax.broadcasted_iota(jnp.int32, (wanted, count), 1)
    hot = (ids[...] * RANK + (r & (RANK - 1)) == c).astype(F32).astype(BF)
    chosen_z = dot_nn(hot, jnp.concatenate([z, z], axis=1))
    chosen_q = dot_nn(hot, jnp.concatenate([q, q], axis=1))
    each = wanted // ways
    for i in range(ways):
        at = i * each
        first = chosen_q[at : at + each // 2]
        second = chosen_q[at + each // 2 : at + each]
        mine = jnp.where(core[0] == 0, first, second)
        picked[i] = jnp.concatenate(
            [side_by_side(chosen_z[at : at + each]), side_by_side(mine)], axis=0
        ).astype(BF)
    hidden_out[...] = dot_nt(numer, prompts[...])
    gram_out[...] = dot_nt(numer, numer)


def join_body(core, parts, hidden, gram, out):
    total = summed(parts)
    size = gram.shape[1]
    cut = total.shape[0] * 2 // 3
    z = one_below_other(total[:cut])
    q = one_below_other(total[cut:])
    none = jnp.zeros_like(q)
    q = jnp.where(
        core[0] == 0, jnp.concatenate([q, none], axis=0), jnp.concatenate([none, q], axis=0)
    )
    out[...] = jnp.concatenate([hidden[...], z, q, gram[...]], axis=1)


def serve_body(a, b, c, d, basis, out):
    total = added((a, b, c, d))
    size = total.shape[0]
    rows = out.shape[0]
    asked = size // RANK
    each = rows // asked
    z = total[:, rows : rows + size]
    q = a[:, rows + size : rows + 2 * size]
    z_high = z.astype(BF)
    z_low = (z - z_high.astype(F32)).astype(BF)
    crossed = []
    for j in range(asked):
        take = slice(j * RANK, (j + 1) * RANK)
        crossed.append(dot_tn(q[take], z_high[take]) + dot_tn(q[take], z_low[take]))
    inverse = inverse_factor(split_gram(total, rows + 2 * size, size))
    cores = in_three(dot_nt, jnp.concatenate(crossed, axis=0), inverse).astype(BF)
    hidden = in_three(dot_nn, inverse, total[:, :rows]).astype(BF)
    for j in range(asked):
        core = cores[j * size : (j + 1) * size]
        mixed = dot_nn(core, hidden[:, j * each : (j + 1) * each]).astype(BF)
        out[j * each : (j + 1) * each, :] = dot_tn(mixed, basis[...]).astype(BF)


def around_y(value, d):
    size = lax.axis_size("feature")
    return lax.ppermute(value, "feature", [(i, (i + d * CORES) % size) for i in range(size)])


def other_core(value):
    size = lax.axis_size("feature")
    return lax.ppermute(value, "feature", [(i, i ^ 1) for i in range(size)])


def over_feature(value, gram_size):
    rows, lanes = value.shape
    pair = call(pair_body, shape((rows, lanes + gram_size), BF), value, other_core(value))
    return [pair] + [around_y(pair, d) for d in (1, 3, 2)]


def on_device(adapter_down, adapter_up, fisher, init_v, init_u, prompt_rows, request_ids):
    ways = lax.axis_size("adapter")
    width = adapter_down.shape[-1]
    size = init_v.shape[1]
    down = adapter_down.reshape(-1, width)
    up = adapter_up.reshape(-1, width)
    count = down.shape[0]
    rows = prompt_rows.shape[0]
    blocks = request_ids.shape[0]
    position = lax.axis_index("adapter")
    fisher_row = jnp.repeat(fisher, RANK)[None, :]
    tile = (size * width // ways // 128, 128)
    tile_shape = shape((ways, *tile), BF)
    flat = shape((size, count), F32)
    digits = jnp.stack([request_ids // RANK, request_ids % RANK]).astype(BF)
    id_tile = lax.dynamic_update_slice(jnp.zeros(tile, BF), digits, (0, position * blocks))

    def swap(parts):
        return lax.all_to_all(parts, "adapter", 0, 0, tiled=True)

    def reduced(tiles):
        return swap(call(sum_body, tile_shape, swap(tiles)))

    def projected(numer, stack):
        value = call(project_body, shape((size, count + size), F32), numer, stack)
        return over_feature(value, size)

    value = call(
        start_body,
        shape((size, 2 * count), F32),
        down,
        up,
        init_v.T.astype(BF),
        init_u.T.astype(BF),
    )
    tiles, q, p = call(
        first_body, [tile_shape, flat, flat], *over_feature(value, 0), up, fisher_row
    )
    for sweep in range(SWEEPS):
        if sweep == 0:
            copies = call(
                sum_ids_body, shape((ways, 2 * tile[0], 128), BF), swap(tiles), id_tile
            )
            value, every_id = call(
                project_ids_body,
                [shape((size, count + size), F32), shape((1, 128), jnp.int32)],
                swap(copies),
                up,
            )
            parts = over_feature(value, size)
        else:
            numer = reduced(tiles)
            parts = projected(numer, up)
        if sweep < SWEEPS - 1:
            tiles, q = call(renew_body, [tile_shape, flat], *parts, p, down, fisher_row)
            parts = projected(reduced(tiles), down)
            tiles, p = call(renew_body, [tile_shape, flat], *parts, q, up, fisher_row)
        else:
            tiles, q, basis = call(
                last_renew_body,
                [tile_shape, flat, shape((size, width), BF)],
                *parts,
                p,
                down,
                fisher_row,
                numer,
            )
    pick_rows = jnp.repeat(every_id[0, : ways * blocks] - position * fisher.shape[0], RANK)[:, None]
    core = jnp.full((1,), lax.axis_index("feature") % CORES, jnp.int32)
    packed = blocks * RANK * 3 // 4
    picked, hidden, gram = call(
        pick_body,
        [shape((ways, packed, 2 * size), BF), shape((size, rows), F32), shape((size, size), F32)],
        core,
        reduced(tiles),
        down,
        prompt_rows,
        q,
        pick_rows,
    )
    value = call(
        join_body, shape((size, rows + 3 * size), F32), core, swap(picked), hidden, gram
    )
    return call(serve_body, shape((rows, width), BF), *over_feature(value, size), basis)


def solution(mesh):
    placed = (
        P("adapter", None, "feature"),
        P("adapter", None, "feature"),
        P("adapter"),
        P("feature", None),
        P("feature", None),
        P("adapter", "feature"),
        P("adapter"),
    )
    return jax.shard_map(
        on_device, mesh=mesh, in_specs=placed, out_specs=P("adapter", "feature"), check_vma=False
    )
```

```python
import jax
import jax.numpy as jnp
from jax import lax
from jax.experimental import pallas as pl
from jax.experimental.pallas import tpu as pltpu
from jax.sharding import PartitionSpec as P

SWEEPS = 3
RANK = 16
CORES = 2
BF = jnp.bfloat16
F32 = jnp.float32


def call(body, outs, *args):
    whole = pl.BlockSpec(memory_space=pltpu.VMEM)
    scalar = pl.BlockSpec(memory_space=pltpu.SMEM)
    single = not isinstance(outs, (list, tuple))
    return pl.pallas_call(
        body,
        out_shape=outs,
        in_specs=[scalar if arg.shape == (1,) else whole for arg in args],
        out_specs=whole if single else [whole] * len(outs),
        compiler_params=pltpu.CompilerParams(vmem_limit_bytes=40 * 1024 * 1024),
    )(*args)


def shape(dims, dtype):
    return jax.ShapeDtypeStruct(dims, dtype)


def dot_nt(a, b, precision=None):
    return lax.dot_general(
        a, b, (((1,), (1,)), ((), ())), preferred_element_type=F32, precision=precision
    )


def dot_tn(a, b, precision=None):
    return lax.dot_general(
        a, b, (((0,), (0,)), ((), ())), preferred_element_type=F32, precision=precision
    )


def dot_nn(a, b, precision=None):
    return jnp.dot(a, b, preferred_element_type=F32, precision=precision)


def in_three(product, a, b):
    a_high, b_high = a.astype(BF), b.astype(BF)
    a_low = (a - a_high.astype(F32)).astype(BF)
    b_low = (b - b_high.astype(F32)).astype(BF)
    return product(a_high, b_high) + (product(a_high, b_low) + product(a_low, b_high))


def inverse_factor(gram):
    size = gram.shape[0]
    rows = lax.broadcasted_iota(jnp.int32, (size, size), 0)
    lanes = lax.broadcasted_iota(jnp.int32, (size, size), 1)
    eye = rows == lanes
    diagonal = jnp.where(eye, gram, 0.0)
    by_row = lax.rsqrt(jnp.sum(diagonal, axis=1, keepdims=True))
    by_lane = lax.rsqrt(jnp.sum(diagonal, axis=0, keepdims=True))
    work = jnp.concatenate([gram * by_row * by_lane, eye.astype(F32)], axis=1)
    group = 8
    whole = (group, 2 * size)
    blocks = [work[group * i : group * (i + 1)] for i in range(size // group)]
    within = lax.broadcasted_iota(jnp.int32, whole, 0)
    for b in range(len(blocks)):
        first = group * b
        columns = [
            {
                j: jnp.broadcast_to(blocks[j][:, first + m : first + m + 1], whole)
                for j in range(b, len(blocks))
            }
            for m in range(group)
        ]
        pivot_rows = [blocks[b][i : i + 1] for i in range(group)]
        pivots = {
            (i, m): columns[m][b][i : i + 1] for i in range(group) for m in range(i, group)
        }
        solved = []
        for p in range(0, group, 2):
            top, mix, low = pivots[p, p], pivots[p, p + 1], pivots[p + 1, p + 1]
            over = 1.0 / (top * low - mix * mix)
            a, b01, c = low * over, -mix * over, top * over
            factors = []
            for i in range(p + 2, group):
                x, y = pivots[p, i], pivots[p + 1, i]
                factors.append((i, a * x + b01 * y, b01 * x + c * y))
            for i, u, v in factors:
                for m in range(i, group):
                    pivots[i, m] = pivots[i, m] - (u * pivots[p, m] + v * pivots[p + 1, m])
                pivot_rows[i] = pivot_rows[i] - (u * pivot_rows[p] + v * pivot_rows[p + 1])
            solved.append((a, b01, c, factors))
        terms = [None] * group
        for p in range(group - 2, -1, -2):
            a, b01, c, factors = solved[p // 2]
            t0 = a * pivot_rows[p] + b01 * pivot_rows[p + 1]
            t1 = b01 * pivot_rows[p] + c * pivot_rows[p + 1]
            for i, u, v in factors:
                t0 = t0 - u * terms[i]
                t1 = t1 - v * terms[i]
            terms[p], terms[p + 1] = t0, t1
        for j in range(b + 1, len(blocks)):
            for m in range(group):
                blocks[j] = blocks[j] - columns[m][j] * terms[m]
        done = blocks[b]
        for p in range(0, group, 2):
            second = pivot_rows[p + 1] - (pivots[p, p + 1] / pivots[p, p]) * pivot_rows[p]
            done = jnp.where(within == p, pivot_rows[p], done)
            done = jnp.where(within == p + 1, second, done)
        blocks[b] = done
    work = jnp.concatenate(blocks, axis=0)
    diagonal = jnp.sum(jnp.where(eye, work[:, :size], 0.0), axis=1, keepdims=True)
    return work[:, size:] * lax.rsqrt(diagonal) * by_lane


def write_copies(ref, value):
    for i in range(ref.shape[0]):
        ref[i] = value


def halves(gram):
    high = gram.astype(BF)
    low = (gram - high.astype(F32)).astype(BF)
    return jnp.concatenate([high, low], axis=1)


def weighted_terms(fresh, other, fisher_row):
    count = fresh.shape[1]
    inner = in_three(dot_tn, fresh, fresh)
    a = lax.broadcasted_iota(jnp.int32, (count, count), 0) // RANK
    b = lax.broadcasted_iota(jnp.int32, (count, count), 1) // RANK
    inner = jnp.where(a == b, inner, 0.0)
    return (in_three(dot_nn, other, inner) * fisher_row).astype(BF)


def added(refs):
    total = refs[0][...].astype(F32)
    for ref in refs[1:]:
        total = total + ref[...].astype(F32)
    return total


def write_tiles(ref, value):
    across = value.shape[1] // 128
    for i in range(ref.shape[0]):
        r, c = divmod(i, across)
        ref[i] = value[16 * r : 16 * r + 16, 128 * c : 128 * c + 128].astype(BF)


def read_tiles(ref, width):
    across = width // 128
    down = ref.shape[0] // across
    return jnp.concatenate(
        [
            jnp.concatenate([ref[r * across + c, :16] for c in range(across)], axis=1)
            for r in range(down)
        ],
        axis=0,
    )


def start_body(down, up, vt, ut, out):
    q = dot_nt(ut[...], up[...])
    p = dot_nt(vt[...], down[...])
    out[...] = jnp.concatenate([q, p], axis=1)


def pair_body(own, got, out):
    total = own[...] + got[...]
    plain = 2 * total.shape[1] - out.shape[1]
    if plain == total.shape[1]:
        out[...] = total.astype(BF)
    else:
        out[...] = jnp.concatenate([total[:, :plain].astype(BF), halves(total[:, plain:])], axis=1)


def first_body(a, b, c, d, stack, fisher_row, tiles, q_out, p_out):
    total = added((a, b, c, d))
    count = total.shape[1] // 2
    q, p = total[:, :count], total[:, count:]
    q_out[...] = q
    p_out[...] = p
    terms = weighted_terms(p, q, fisher_row[...])
    write_tiles(tiles, dot_nn(terms, stack[...]))


def summed(ref):
    total = ref[0].astype(F32)
    for i in range(1, ref.shape[0]):
        total = total + ref[i].astype(F32)
    return total


def sum_body(parts, out):
    write_copies(out, summed(parts).astype(BF))


def sum_ids_body(parts, ids, out):
    write_copies(out, jnp.concatenate([summed(parts).astype(BF), ids[...]], axis=0))


def project_body(tiles, stack, out):
    numer = read_tiles(tiles, stack.shape[1])
    out[...] = jnp.concatenate([dot_nt(numer, stack[...]), dot_nt(numer, numer)], axis=1)


def project_ids_body(tiles, stack, out, ids_out):
    project_body(tiles, stack, out)
    ids = summed(tiles.at[:, 16:])
    ids_out[...] = (ids[0:1] * RANK + ids[1:2]).astype(jnp.int32)


def split_gram(total, at, size):
    return total[:, at : at + size] + total[:, at + size : at + 2 * size]


def renew(parts, other, stack, fisher_row, tiles, fresh_out):
    total = added(parts)
    size, count = other.shape
    inverse = inverse_factor(split_gram(total, count, size))
    fresh = in_three(dot_nn, inverse, total[:, :count])
    fresh_out[...] = fresh
    terms = weighted_terms(fresh, other[...], fisher_row[...])
    write_tiles(tiles, dot_nn(terms, stack[...]))
    return inverse


def renew_body(a, b, c, d, other, stack, fisher_row, tiles, fresh_out):
    renew((a, b, c, d), other, stack, fisher_row, tiles, fresh_out)


def last_renew_body(
    a, b, c, d, other, stack, fisher_row, numer_tiles, tiles, fresh_out, basis_out
):
    inverse = renew((a, b, c, d), other, stack, fisher_row, tiles, fresh_out)
    numer = read_tiles(numer_tiles, stack.shape[1]).astype(F32)
    basis_out[...] = in_three(dot_nn, inverse, numer).astype(BF)


def side_by_side(value):
    half = value.shape[0] // 2
    lanes = lax.broadcasted_iota(jnp.int32, (half, value.shape[1]), 1)
    return jnp.where(lanes < value.shape[1] // 2, value[:half], value[half:])


def one_below_other(value):
    half = value.shape[1] // 2
    return jnp.concatenate([value[:, :half], value[:, half:]], axis=0)


def pick_body(core, tiles, stack, prompts, q_ref, ids, picked, hidden_out, gram_out):
    numer = read_tiles(tiles, stack.shape[1])
    z = dot_nt(stack[...], numer).astype(BF)
    q = q_ref[...].T.astype(BF)
    count, size = z.shape
    ways = picked.shape[0]
    wanted = ids.shape[0]
    r = lax.broadcasted_iota(jnp.int32, (wanted, count), 0)
    c = lax.broadcasted_iota(jnp.int32, (wanted, count), 1)
    hot = (ids[...] * RANK + (r & (RANK - 1)) == c).astype(F32).astype(BF)
    chosen = dot_nn(hot, jnp.concatenate([z, z, q, q], axis=1))
    chosen_z, chosen_q = chosen[:, : 2 * size], chosen[:, 2 * size :]
    each = wanted // ways
    for i in range(ways):
        at = i * each
        first = chosen_q[at : at + each // 2]
        second = chosen_q[at + each // 2 : at + each]
        mine = jnp.where(core[0] == 0, first, second)
        picked[i] = jnp.concatenate(
            [side_by_side(chosen_z[at : at + each]), side_by_side(mine)], axis=0
        ).astype(BF)
    hidden_out[...] = dot_nt(numer, prompts[...])
    gram_out[...] = dot_nt(numer, numer)


def join_body(core, parts, hidden, gram, out):
    total = summed(parts)
    size = gram.shape[1]
    cut = total.shape[0] * 2 // 3
    z = one_below_other(total[:cut])
    q = one_below_other(total[cut:])
    none = jnp.zeros_like(q)
    q = jnp.where(
        core[0] == 0, jnp.concatenate([q, none], axis=0), jnp.concatenate([none, q], axis=0)
    )
    out[...] = jnp.concatenate([hidden[...], z, q, gram[...]], axis=1)


def serve_body(a, b, c, d, basis, out):
    total = added((a, b, c, d))
    size = total.shape[0]
    rows = out.shape[0]
    asked = size // RANK
    each = rows // asked
    z = total[:, rows : rows + size]
    q = a[:, rows + size : rows + 2 * size]
    z_high = z.astype(BF)
    z_low = (z - z_high.astype(F32)).astype(BF)
    crossed = []
    for j in range(asked):
        take = slice(j * RANK, (j + 1) * RANK)
        crossed.append(dot_tn(q[take], z_high[take]) + dot_tn(q[take], z_low[take]))
    inverse = inverse_factor(split_gram(total, rows + 2 * size, size))
    cores = in_three(dot_nt, jnp.concatenate(crossed, axis=0), inverse).astype(BF)
    hidden = in_three(dot_nn, inverse, total[:, :rows]).astype(BF)
    for j in range(asked):
        core = cores[j * size : (j + 1) * size]
        mixed = dot_nn(core, hidden[:, j * each : (j + 1) * each]).astype(BF)
        out[j * each : (j + 1) * each, :] = dot_tn(mixed, basis[...]).astype(BF)


def around_y(value, d):
    size = lax.axis_size("feature")
    return lax.ppermute(value, "feature", [(i, (i + d * CORES) % size) for i in range(size)])


def other_core(value):
    size = lax.axis_size("feature")
    return lax.ppermute(value, "feature", [(i, i ^ 1) for i in range(size)])


def over_feature(value, gram_size):
    rows, lanes = value.shape
    pair = call(pair_body, shape((rows, lanes + gram_size), BF), value, other_core(value))
    return [pair] + [around_y(pair, d) for d in (1, 2, 3)]


def on_device(adapter_down, adapter_up, fisher, init_v, init_u, prompt_rows, request_ids):
    ways = lax.axis_size("adapter")
    width = adapter_down.shape[-1]
    size = init_v.shape[1]
    down = adapter_down.reshape(-1, width)
    up = adapter_up.reshape(-1, width)
    count = down.shape[0]
    rows = prompt_rows.shape[0]
    blocks = request_ids.shape[0]
    position = lax.axis_index("adapter")
    fisher_row = jnp.repeat(fisher, RANK)[None, :]
    tile = (size * width // ways // 128, 128)
    tile_shape = shape((ways, *tile), BF)
    flat = shape((size, count), F32)
    digits = jnp.stack([request_ids // RANK, request_ids % RANK]).astype(BF)
    id_tile = lax.dynamic_update_slice(jnp.zeros(tile, BF), digits, (0, position * blocks))

    def swap(parts):
        return lax.all_to_all(parts, "adapter", 0, 0, tiled=True)

    def reduced(tiles):
        return swap(call(sum_body, tile_shape, swap(tiles)))

    def projected(numer, stack):
        value = call(project_body, shape((size, count + size), F32), numer, stack)
        return over_feature(value, size)

    value = call(
        start_body,
        shape((size, 2 * count), F32),
        down,
        up,
        init_v.T.astype(BF),
        init_u.T.astype(BF),
    )
    tiles, q, p = call(
        first_body, [tile_shape, flat, flat], *over_feature(value, 0), up, fisher_row
    )
    for sweep in range(SWEEPS):
        if sweep == 0:
            copies = call(
                sum_ids_body, shape((ways, 2 * tile[0], 128), BF), swap(tiles), id_tile
            )
            value, every_id = call(
                project_ids_body,
                [shape((size, count + size), F32), shape((1, 128), jnp.int32)],
                swap(copies),
                up,
            )
            parts = over_feature(value, size)
        else:
            numer = reduced(tiles)
            parts = projected(numer, up)
        if sweep < SWEEPS - 1:
            tiles, q = call(renew_body, [tile_shape, flat], *parts, p, down, fisher_row)
            parts = projected(reduced(tiles), down)
            tiles, p = call(renew_body, [tile_shape, flat], *parts, q, up, fisher_row)
        else:
            tiles, q, basis = call(
                last_renew_body,
                [tile_shape, flat, shape((size, width), BF)],
                *parts,
                p,
                down,
                fisher_row,
                numer,
            )
    pick_rows = jnp.repeat(every_id[0, : ways * blocks] - position * fisher.shape[0], RANK)[:, None]
    core = jnp.full((1,), lax.axis_index("feature") % CORES, jnp.int32)
    packed = blocks * RANK * 3 // 4
    picked, hidden, gram = call(
        pick_body,
        [shape((ways, packed, 2 * size), BF), shape((size, rows), F32), shape((size, size), F32)],
        core,
        reduced(tiles),
        down,
        prompt_rows,
        q,
        pick_rows,
    )
    value = call(
        join_body, shape((size, rows + 3 * size), F32), core, swap(picked), hidden, gram
    )
    return call(serve_body, shape((rows, width), BF), *over_feature(value, size), basis)


def solution(mesh):
    placed = (
        P("adapter", None, "feature"),
        P("adapter", None, "feature"),
        P("adapter"),
        P("feature", None),
        P("feature", None),
        P("adapter", "feature"),
        P("adapter"),
    )
    return jax.shard_map(
        on_device, mesh=mesh, in_specs=placed, out_specs=P("adapter", "feature"), check_vma=False
    )
```

```python
import jax
import jax.numpy as jnp
from jax import lax
from jax.experimental import pallas as pl
from jax.experimental.pallas import tpu as pltpu
from jax.sharding import PartitionSpec as P

SWEEPS = 3
RANK = 16
CORES, CHIPS = 2, 4
BF = jnp.bfloat16
F32 = jnp.float32


def call(body, outs, *args):
    whole = pl.BlockSpec(memory_space=pltpu.VMEM)
    scalar = pl.BlockSpec(memory_space=pltpu.SMEM)
    single = not isinstance(outs, (list, tuple))
    return pl.pallas_call(
        body,
        out_shape=outs,
        in_specs=[scalar if arg.shape == (1,) else whole for arg in args],
        out_specs=whole if single else [whole] * len(outs),
        compiler_params=pltpu.CompilerParams(vmem_limit_bytes=40 * 1024 * 1024),
    )(*args)


def shape(dims, dtype):
    return jax.ShapeDtypeStruct(dims, dtype)


def dot_nt(a, b, precision=None):
    return lax.dot_general(
        a, b, (((1,), (1,)), ((), ())), preferred_element_type=F32, precision=precision
    )


def dot_tn(a, b, precision=None):
    return lax.dot_general(
        a, b, (((0,), (0,)), ((), ())), preferred_element_type=F32, precision=precision
    )


def dot_nn(a, b, precision=None):
    return jnp.dot(a, b, preferred_element_type=F32, precision=precision)


def in_three(product, a, b):
    a_high, b_high = a.astype(BF), b.astype(BF)
    a_low = (a - a_high.astype(F32)).astype(BF)
    b_low = (b - b_high.astype(F32)).astype(BF)
    return product(a_high, b_high) + (product(a_high, b_low) + product(a_low, b_high))


def inverse_factor(gram):
    size = gram.shape[0]
    rows = lax.broadcasted_iota(jnp.int32, (size, size), 0)
    lanes = lax.broadcasted_iota(jnp.int32, (size, size), 1)
    eye = rows == lanes
    diagonal = jnp.where(eye, gram, 0.0)
    by_row = lax.rsqrt(jnp.sum(diagonal, axis=1, keepdims=True))
    by_lane = lax.rsqrt(jnp.sum(diagonal, axis=0, keepdims=True))
    work = jnp.concatenate([gram * by_row * by_lane, eye.astype(F32)], axis=1)
    group = 8
    whole = (group, 2 * size)
    blocks = [work[group * i : group * (i + 1)] for i in range(size // group)]
    within = lax.broadcasted_iota(jnp.int32, whole, 0)
    for b in range(len(blocks)):
        first = group * b
        columns = [
            {
                j: jnp.broadcast_to(blocks[j][:, first + m : first + m + 1], whole)
                for j in range(b, len(blocks))
            }
            for m in range(group)
        ]
        pivot_rows = [blocks[b][i : i + 1] for i in range(group)]
        pivots = {
            (i, m): columns[m][b][i : i + 1] for i in range(group) for m in range(i, group)
        }
        solved = []
        for p in range(0, group, 2):
            top, mix, low = pivots[p, p], pivots[p, p + 1], pivots[p + 1, p + 1]
            over = 1.0 / (top * low - mix * mix)
            a, b01, c = low * over, -mix * over, top * over
            factors = []
            for i in range(p + 2, group):
                x, y = pivots[p, i], pivots[p + 1, i]
                factors.append((i, a * x + b01 * y, b01 * x + c * y))
            for i, u, v in factors:
                for m in range(i, group):
                    pivots[i, m] = pivots[i, m] - (u * pivots[p, m] + v * pivots[p + 1, m])
                pivot_rows[i] = pivot_rows[i] - (u * pivot_rows[p] + v * pivot_rows[p + 1])
            solved.append((a, b01, c, factors))
        terms = [None] * group
        for p in range(group - 2, -1, -2):
            a, b01, c, factors = solved[p // 2]
            t0 = a * pivot_rows[p] + b01 * pivot_rows[p + 1]
            t1 = b01 * pivot_rows[p] + c * pivot_rows[p + 1]
            for i, u, v in factors:
                t0 = t0 - u * terms[i]
                t1 = t1 - v * terms[i]
            terms[p], terms[p + 1] = t0, t1
        for j in range(b + 1, len(blocks)):
            for m in range(group):
                blocks[j] = blocks[j] - columns[m][j] * terms[m]
        done = blocks[b]
        for p in range(0, group, 2):
            second = pivot_rows[p + 1] - (pivots[p, p + 1] / pivots[p, p]) * pivot_rows[p]
            done = jnp.where(within == p, pivot_rows[p], done)
            done = jnp.where(within == p + 1, second, done)
        blocks[b] = done
    work = jnp.concatenate(blocks, axis=0)
    diagonal = jnp.sum(jnp.where(eye, work[:, :size], 0.0), axis=1, keepdims=True)
    return work[:, size:] * lax.rsqrt(diagonal) * by_lane


def write_copies(ref, value):
    for i in range(ref.shape[0]):
        ref[i] = value


def halves(gram):
    high = gram.astype(BF)
    low = (gram - high.astype(F32)).astype(BF)
    return jnp.concatenate([high, low], axis=1)


def weighted_terms(fresh, other, fisher_row):
    count = fresh.shape[1]
    inner = in_three(dot_tn, fresh, fresh)
    a = lax.broadcasted_iota(jnp.int32, (count, count), 0) // RANK
    b = lax.broadcasted_iota(jnp.int32, (count, count), 1) // RANK
    inner = jnp.where(a == b, inner, 0.0)
    return (in_three(dot_nn, other, inner) * fisher_row).astype(BF)


def added(refs):
    total = refs[0][...].astype(F32)
    for ref in refs[1:]:
        total = total + ref[...].astype(F32)
    return total


def write_tiles(ref, value):
    across = value.shape[1] // 128
    for i in range(ref.shape[0]):
        r, c = divmod(i, across)
        ref[i] = value[16 * r : 16 * r + 16, 128 * c : 128 * c + 128].astype(BF)


def read_tiles(ref, width):
    across = width // 128
    down = ref.shape[0] // across
    return jnp.concatenate(
        [
            jnp.concatenate([ref[r * across + c, :16] for c in range(across)], axis=1)
            for r in range(down)
        ],
        axis=0,
    )


def start_body(down, up, vt, ut, out):
    q = dot_nt(ut[...], up[...])
    p = dot_nt(vt[...], down[...])
    out[...] = jnp.concatenate([q, p], axis=1).astype(BF)


def along_y_body(a, b, c, d, out):
    total = added((a, b, c, d))
    extra = total.shape[1] - out.shape[1]
    if extra:
        plain = out.shape[1] - extra
        gram = total[:, plain : plain + extra] + total[:, plain + extra :]
        total = jnp.concatenate([total[:, :plain], gram], axis=1)
    out[...] = total


def first_body(own, got, stack, fisher_row, tiles, q_out, p_out):
    total = own[...] + got[...]
    count = total.shape[1] // 2
    q, p = total[:, :count], total[:, count:]
    q_out[...] = q
    p_out[...] = p
    terms = weighted_terms(p, q, fisher_row[...])
    write_tiles(tiles, dot_nn(terms, stack[...]))


def summed(ref):
    total = ref[0].astype(F32)
    for i in range(1, ref.shape[0]):
        total = total + ref[i].astype(F32)
    return total


def sum_body(parts, out):
    write_copies(out, summed(parts).astype(BF))


def sum_ids_body(parts, ids, out):
    write_copies(out, jnp.concatenate([summed(parts).astype(BF), ids[...]], axis=0))


def project_body(tiles, stack, out):
    numer = read_tiles(tiles, stack.shape[1])
    y = dot_nt(numer, stack[...]).astype(BF)
    out[...] = jnp.concatenate([y, halves(dot_nt(numer, numer))], axis=1)


def project_ids_body(tiles, stack, out, ids_out):
    project_body(tiles, stack, out)
    ids = summed(tiles.at[:, 16:])
    ids_out[...] = (ids[0:1] * RANK + ids[1:2]).astype(jnp.int32)


def renew(parts, other, stack, fisher_row, tiles, fresh_out):
    total = parts[0][...] + parts[1][...]
    size, count = other.shape
    inverse = inverse_factor(total[:, count:])
    fresh = in_three(dot_nn, inverse, total[:, :count])
    fresh_out[...] = fresh
    terms = weighted_terms(fresh, other[...], fisher_row[...])
    write_tiles(tiles, dot_nn(terms, stack[...]))
    return inverse


def renew_body(own, got, other, stack, fisher_row, tiles, fresh_out):
    renew((own, got), other, stack, fisher_row, tiles, fresh_out)


def last_renew_body(
    own, got, other, stack, fisher_row, numer_tiles, tiles, fresh_out, basis_out
):
    inverse = renew((own, got), other, stack, fisher_row, tiles, fresh_out)
    numer = read_tiles(numer_tiles, stack.shape[1]).astype(F32)
    basis_out[...] = in_three(dot_nn, inverse, numer).astype(BF)


def side_by_side(value):
    half = value.shape[0] // 2
    lanes = lax.broadcasted_iota(jnp.int32, (half, value.shape[1]), 1)
    return jnp.where(lanes < value.shape[1] // 2, value[:half], value[half:])


def one_below_other(value):
    half = value.shape[1] // 2
    return jnp.concatenate([value[:, :half], value[:, half:]], axis=0)


def pick_body(core, tiles, stack, prompts, q_ref, ids, picked, hidden_out, gram_out):
    numer = read_tiles(tiles, stack.shape[1])
    z = dot_nt(stack[...], numer).astype(BF)
    q = q_ref[...].T.astype(BF)
    count, size = z.shape
    ways = picked.shape[0]
    wanted = ids.shape[0]
    r = lax.broadcasted_iota(jnp.int32, (wanted, count), 0)
    c = lax.broadcasted_iota(jnp.int32, (wanted, count), 1)
    hot = (ids[...] * RANK + (r & (RANK - 1)) == c).astype(F32).astype(BF)
    chosen = dot_nn(hot, jnp.concatenate([z, z, q, q], axis=1))
    chosen_z, chosen_q = chosen[:, : 2 * size], chosen[:, 2 * size :]
    each = wanted // ways
    for i in range(ways):
        at = i * each
        first = chosen_q[at : at + each // 2]
        second = chosen_q[at + each // 2 : at + each]
        mine = jnp.where(core[0] == 0, first, second)
        picked[i] = jnp.concatenate(
            [side_by_side(chosen_z[at : at + each]), side_by_side(mine)], axis=0
        ).astype(BF)
    hidden_out[...] = dot_nt(numer, prompts[...]).astype(BF)
    gram_out[...] = halves(dot_nt(numer, numer))


def join_body(core, parts, hidden, gram, out):
    total = summed(parts)
    cut = total.shape[0] * 2 // 3
    z = one_below_other(total[:cut])
    q = one_below_other(total[cut:]) / CHIPS
    none = jnp.zeros_like(q)
    q = jnp.where(
        core[0] == 0, jnp.concatenate([q, none], axis=0), jnp.concatenate([none, q], axis=0)
    )
    out[...] = jnp.concatenate([hidden[...], z.astype(BF), q.astype(BF), gram[...]], axis=1)


def serve_body(own, got, basis, out):
    total = own[...] + got[...]
    size = total.shape[0]
    rows = out.shape[0]
    asked = size // RANK
    each = rows // asked
    z = total[:, rows : rows + size]
    q = total[:, rows + size : rows + 2 * size].astype(BF)
    z_high = z.astype(BF)
    z_low = (z - z_high.astype(F32)).astype(BF)
    crossed = []
    for j in range(asked):
        take = slice(j * RANK, (j + 1) * RANK)
        crossed.append(dot_tn(q[take], z_high[take]) + dot_tn(q[take], z_low[take]))
    inverse = inverse_factor(total[:, rows + 2 * size :])
    cores = in_three(dot_nt, jnp.concatenate(crossed, axis=0), inverse).astype(BF)
    hidden = in_three(dot_nn, inverse, total[:, :rows]).astype(BF)
    for j in range(asked):
        core = cores[j * size : (j + 1) * size]
        mixed = dot_nn(core, hidden[:, j * each : (j + 1) * each]).astype(BF)
        out[j * each : (j + 1) * each, :] = dot_tn(mixed, basis[...]).astype(BF)


def around_y(value, d):
    size = lax.axis_size("feature")
    return lax.ppermute(value, "feature", [(i, (i + d * CORES) % size) for i in range(size)])


def other_core(value):
    size = lax.axis_size("feature")
    return lax.ppermute(value, "feature", [(i, i ^ 1) for i in range(size)])


def over_feature(value, gram_size):
    rows, lanes = value.shape
    parts = [value] + [around_y(value, d) for d in (1, 3, 2)]
    chips = call(along_y_body, shape((rows, lanes - gram_size), F32), *parts)
    return [chips, other_core(chips)]


def on_device(adapter_down, adapter_up, fisher, init_v, init_u, prompt_rows, request_ids):
    ways = lax.axis_size("adapter")
    width = adapter_down.shape[-1]
    size = init_v.shape[1]
    down = adapter_down.reshape(-1, width)
    up = adapter_up.reshape(-1, width)
    count = down.shape[0]
    rows = prompt_rows.shape[0]
    blocks = request_ids.shape[0]
    position = lax.axis_index("adapter")
    fisher_row = jnp.repeat(fisher, RANK)[None, :]
    tile = (size * width // ways // 128, 128)
    tile_shape = shape((ways, *tile), BF)
    flat = shape((size, count), F32)
    digits = jnp.stack([request_ids // RANK, request_ids % RANK]).astype(BF)
    id_tile = lax.dynamic_update_slice(jnp.zeros(tile, BF), digits, (0, position * blocks))

    def swap(parts):
        return lax.all_to_all(parts, "adapter", 0, 0, tiled=True)

    def reduced(tiles):
        return swap(call(sum_body, tile_shape, swap(tiles)))

    def projected(numer, stack):
        value = call(project_body, shape((size, count + 2 * size), BF), numer, stack)
        return over_feature(value, size)

    value = call(
        start_body,
        shape((size, 2 * count), BF),
        down,
        up,
        init_v.T.astype(BF),
        init_u.T.astype(BF),
    )
    tiles, q, p = call(
        first_body, [tile_shape, flat, flat], *over_feature(value, 0), up, fisher_row
    )
    for sweep in range(SWEEPS):
        if sweep == 0:
            copies = call(
                sum_ids_body, shape((ways, 2 * tile[0], 128), BF), swap(tiles), id_tile
            )
            value, every_id = call(
                project_ids_body,
                [shape((size, count + 2 * size), BF), shape((1, 128), jnp.int32)],
                swap(copies),
                up,
            )
            parts = over_feature(value, size)
        else:
            numer = reduced(tiles)
            parts = projected(numer, up)
        if sweep < SWEEPS - 1:
            tiles, q = call(renew_body, [tile_shape, flat], *parts, p, down, fisher_row)
            parts = projected(reduced(tiles), down)
            tiles, p = call(renew_body, [tile_shape, flat], *parts, q, up, fisher_row)
        else:
            tiles, q, basis = call(
                last_renew_body,
                [tile_shape, flat, shape((size, width), BF)],
                *parts,
                p,
                down,
                fisher_row,
                numer,
            )
    pick_rows = jnp.repeat(every_id[0, : ways * blocks] - position * fisher.shape[0], RANK)[:, None]
    core = jnp.full((1,), lax.axis_index("feature") % CORES, jnp.int32)
    packed = blocks * RANK * 3 // 4
    picked, hidden, gram = call(
        pick_body,
        [shape((ways, packed, 2 * size), BF), shape((size, rows), BF), shape((size, 2 * size), BF)],
        core,
        reduced(tiles),
        down,
        prompt_rows,
        q,
        pick_rows,
    )
    value = call(
        join_body, shape((size, rows + 4 * size), BF), core, swap(picked), hidden, gram
    )
    return call(serve_body, shape((rows, width), BF), *over_feature(value, size), basis)


def solution(mesh):
    placed = (
        P("adapter", None, "feature"),
        P("adapter", None, "feature"),
        P("adapter"),
        P("feature", None),
        P("feature", None),
        P("adapter", "feature"),
        P("adapter"),
    )
    return jax.shard_map(
        on_device, mesh=mesh, in_specs=placed, out_specs=P("adapter", "feature"), check_vma=False
    )
```

```python
import jax
import jax.numpy as jnp
from jax import lax
from jax.experimental import pallas as pl
from jax.experimental.pallas import tpu as pltpu
from jax.sharding import PartitionSpec as P

SWEEPS = 3
RANK = 16
CORES = 2
BF = jnp.bfloat16
F32 = jnp.float32


def call(body, outs, *args):
    whole = pl.BlockSpec(memory_space=pltpu.VMEM)
    scalar = pl.BlockSpec(memory_space=pltpu.SMEM)
    single = not isinstance(outs, (list, tuple))
    return pl.pallas_call(
        body,
        out_shape=outs,
        in_specs=[scalar if arg.shape == (1,) else whole for arg in args],
        out_specs=whole if single else [whole] * len(outs),
        compiler_params=pltpu.CompilerParams(vmem_limit_bytes=40 * 1024 * 1024),
    )(*args)


def shape(dims, dtype):
    return jax.ShapeDtypeStruct(dims, dtype)


def dot_nt(a, b, precision=None):
    return lax.dot_general(
        a, b, (((1,), (1,)), ((), ())), preferred_element_type=F32, precision=precision
    )


def dot_tn(a, b, precision=None):
    return lax.dot_general(
        a, b, (((0,), (0,)), ((), ())), preferred_element_type=F32, precision=precision
    )


def dot_nn(a, b, precision=None):
    return jnp.dot(a, b, preferred_element_type=F32, precision=precision)


def in_three(product, a, b):
    a_high, b_high = a.astype(BF), b.astype(BF)
    a_low = (a - a_high.astype(F32)).astype(BF)
    b_low = (b - b_high.astype(F32)).astype(BF)
    return product(a_high, b_high) + (product(a_high, b_low) + product(a_low, b_high))


def inverse_factor(gram):
    size = gram.shape[0]
    rows = lax.broadcasted_iota(jnp.int32, (size, size), 0)
    lanes = lax.broadcasted_iota(jnp.int32, (size, size), 1)
    eye = rows == lanes
    diagonal = jnp.where(eye, gram, 0.0)
    by_row = lax.rsqrt(jnp.sum(diagonal, axis=1, keepdims=True))
    by_lane = lax.rsqrt(jnp.sum(diagonal, axis=0, keepdims=True))
    work = jnp.concatenate([gram * by_row * by_lane, eye.astype(F32)], axis=1)
    group = 8
    whole = (group, 2 * size)
    blocks = [work[group * i : group * (i + 1)] for i in range(size // group)]
    within = lax.broadcasted_iota(jnp.int32, whole, 0)
    for b in range(len(blocks)):
        first = group * b
        columns = [
            {
                j: jnp.broadcast_to(blocks[j][:, first + m : first + m + 1], whole)
                for j in range(b, len(blocks))
            }
            for m in range(group)
        ]
        pivot_rows = [blocks[b][i : i + 1] for i in range(group)]
        pivots = {
            (i, m): columns[m][b][i : i + 1] for i in range(group) for m in range(i, group)
        }
        solved = []
        for p in range(0, group, 2):
            top, mix, low = pivots[p, p], pivots[p, p + 1], pivots[p + 1, p + 1]
            over = 1.0 / (top * low - mix * mix)
            a, b01, c = low * over, -mix * over, top * over
            factors = []
            for i in range(p + 2, group):
                x, y = pivots[p, i], pivots[p + 1, i]
                factors.append((i, a * x + b01 * y, b01 * x + c * y))
            for i, u, v in factors:
                for m in range(i, group):
                    pivots[i, m] = pivots[i, m] - (u * pivots[p, m] + v * pivots[p + 1, m])
                pivot_rows[i] = pivot_rows[i] - (u * pivot_rows[p] + v * pivot_rows[p + 1])
            solved.append((a, b01, c, factors))
        terms = [None] * group
        for p in range(group - 2, -1, -2):
            a, b01, c, factors = solved[p // 2]
            t0 = a * pivot_rows[p] + b01 * pivot_rows[p + 1]
            t1 = b01 * pivot_rows[p] + c * pivot_rows[p + 1]
            for i, u, v in factors:
                t0 = t0 - u * terms[i]
                t1 = t1 - v * terms[i]
            terms[p], terms[p + 1] = t0, t1
        for j in range(b + 1, len(blocks)):
            for m in range(group):
                blocks[j] = blocks[j] - columns[m][j] * terms[m]
        done = blocks[b]
        for p in range(0, group, 2):
            second = pivot_rows[p + 1] - (pivots[p, p + 1] / pivots[p, p]) * pivot_rows[p]
            done = jnp.where(within == p, pivot_rows[p], done)
            done = jnp.where(within == p + 1, second, done)
        blocks[b] = done
    work = jnp.concatenate(blocks, axis=0)
    diagonal = jnp.sum(jnp.where(eye, work[:, :size], 0.0), axis=1, keepdims=True)
    return work[:, size:] * lax.rsqrt(diagonal) * by_lane


def write_copies(ref, value):
    for i in range(ref.shape[0]):
        ref[i] = value


def halves(gram):
    high = gram.astype(BF)
    low = (gram - high.astype(F32)).astype(BF)
    return jnp.concatenate([high, low], axis=1)


def weighted_terms(fresh, other, fisher_row):
    count = fresh.shape[1]
    inner = in_three(dot_tn, fresh, fresh)
    a = lax.broadcasted_iota(jnp.int32, (count, count), 0) // RANK
    b = lax.broadcasted_iota(jnp.int32, (count, count), 1) // RANK
    inner = jnp.where(a == b, inner, 0.0)
    return (in_three(dot_nn, other, inner) * fisher_row).astype(BF)


def added(refs):
    total = refs[0][...].astype(F32)
    for ref in refs[1:]:
        total = total + ref[...].astype(F32)
    return total


def write_tiles(ref, value):
    across = value.shape[1] // 128
    for i in range(ref.shape[0]):
        r, c = divmod(i, across)
        ref[i] = value[16 * r : 16 * r + 16, 128 * c : 128 * c + 128].astype(BF)


def read_tiles(ref, width):
    across = width // 128
    down = ref.shape[0] // across
    return jnp.concatenate(
        [
            jnp.concatenate([ref[r * across + c, :16] for c in range(across)], axis=1)
            for r in range(down)
        ],
        axis=0,
    )


def start_body(down, up, vt, ut, out):
    q = dot_nt(ut[...], up[...])
    p = dot_nt(vt[...], down[...])
    out[...] = jnp.concatenate([q, p], axis=1)


def pair_body(own, got, out):
    total = own[...] + got[...]
    plain = 2 * total.shape[1] - out.shape[1]
    if plain == total.shape[1]:
        out[...] = total.astype(BF)
    else:
        out[...] = jnp.concatenate([total[:, :plain].astype(BF), halves(total[:, plain:])], axis=1)


def first_body(a, b, c, d, stack, fisher_row, tiles, q_out, p_out):
    total = added((a, b, c, d))
    count = total.shape[1] // 2
    q, p = total[:, :count], total[:, count:]
    q_out[...] = q
    p_out[...] = p
    terms = weighted_terms(p, q, fisher_row[...])
    write_tiles(tiles, dot_nn(terms, stack[...]))


def summed(ref):
    total = ref[0].astype(F32)
    for i in range(1, ref.shape[0]):
        total = total + ref[i].astype(F32)
    return total


def sum_body(parts, out):
    write_copies(out, summed(parts).astype(BF))


def sum_ids_body(parts, ids, out):
    write_copies(out, jnp.concatenate([summed(parts).astype(BF), ids[...]], axis=0))


def project_body(tiles, stack, out):
    numer = read_tiles(tiles, stack.shape[1])
    out[...] = jnp.concatenate([dot_nt(numer, stack[...]), dot_nt(numer, numer)], axis=1)


def project_ids_body(tiles, stack, out, ids_out):
    project_body(tiles, stack, out)
    ids = summed(tiles.at[:, 16:])
    ids_out[...] = (ids[0:1] * RANK + ids[1:2]).astype(jnp.int32)


def split_gram(total, at, size):
    return total[:, at : at + size] + total[:, at + size : at + 2 * size]


def renew(parts, other, stack, fisher_row, tiles, fresh_out):
    total = added(parts)
    size, count = other.shape
    inverse = inverse_factor(split_gram(total, count, size))
    fresh = in_three(dot_nn, inverse, total[:, :count])
    fresh_out[...] = fresh
    terms = weighted_terms(fresh, other[...], fisher_row[...])
    write_tiles(tiles, dot_nn(terms, stack[...]))
    return inverse


def renew_body(a, b, c, d, other, stack, fisher_row, tiles, fresh_out):
    renew((a, b, c, d), other, stack, fisher_row, tiles, fresh_out)


def last_renew_body(
    a, b, c, d, other, stack, fisher_row, numer_tiles, tiles, fresh_out, basis_out
):
    inverse = renew((a, b, c, d), other, stack, fisher_row, tiles, fresh_out)
    numer = read_tiles(numer_tiles, stack.shape[1]).astype(F32)
    basis_out[...] = in_three(dot_nn, inverse, numer).astype(BF)


def side_by_side(value):
    half = value.shape[0] // 2
    lanes = lax.broadcasted_iota(jnp.int32, (half, value.shape[1]), 1)
    return jnp.where(lanes < value.shape[1] // 2, value[:half], value[half:])


def one_below_other(value):
    half = value.shape[1] // 2
    return jnp.concatenate([value[:, :half], value[:, half:]], axis=0)


def pick_body(core, tiles, stack, prompts, q_ref, ids, picked, hidden_out, gram_out):
    numer = read_tiles(tiles, stack.shape[1])
    z = dot_nt(stack[...], numer).astype(BF)
    q = q_ref[...].T.astype(BF)
    count, size = z.shape
    ways = picked.shape[0]
    wanted = ids.shape[0]
    r = lax.broadcasted_iota(jnp.int32, (wanted, count), 0)
    c = lax.broadcasted_iota(jnp.int32, (wanted, count), 1)
    hot = (ids[...] * RANK + (r & (RANK - 1)) == c).astype(F32).astype(BF)
    chosen = dot_nn(hot, jnp.concatenate([z, z, q, q], axis=1))
    chosen_z, chosen_q = chosen[:, : 2 * size], chosen[:, 2 * size :]
    each = wanted // ways
    for i in range(ways):
        at = i * each
        first = chosen_q[at : at + each // 2]
        second = chosen_q[at + each // 2 : at + each]
        mine = jnp.where(core[0] == 0, first, second)
        picked[i] = jnp.concatenate(
            [side_by_side(chosen_z[at : at + each]), side_by_side(mine)], axis=0
        ).astype(BF)
    hidden_out[...] = dot_nt(numer, prompts[...])
    gram_out[...] = dot_nt(numer, numer)


def join_body(core, parts, hidden, gram, out):
    total = summed(parts)
    size = gram.shape[1]
    cut = total.shape[0] * 2 // 3
    z = one_below_other(total[:cut])
    q = one_below_other(total[cut:])
    none = jnp.zeros_like(q)
    q = jnp.where(
        core[0] == 0, jnp.concatenate([q, none], axis=0), jnp.concatenate([none, q], axis=0)
    )
    out[...] = jnp.concatenate([hidden[...], z, q, gram[...]], axis=1)


def serve_body(a, b, c, d, basis, out, hold, sent):
    total = added((a, b, c, d))
    size = total.shape[0]
    rows = out.shape[0]
    asked = size // RANK
    each = rows // asked
    z = total[:, rows : rows + size]
    q = a[:, rows + size : rows + 2 * size]
    z_high = z.astype(BF)
    z_low = (z - z_high.astype(F32)).astype(BF)
    crossed = []
    for j in range(asked):
        take = slice(j * RANK, (j + 1) * RANK)
        crossed.append(dot_tn(q[take], z_high[take]) + dot_tn(q[take], z_low[take]))
    inverse = inverse_factor(split_gram(total, rows + 2 * size, size))
    cores = in_three(dot_nt, jnp.concatenate(crossed, axis=0), inverse).astype(BF)
    hidden = in_three(dot_nn, inverse, total[:, :rows]).astype(BF)
    copies = []
    for j in range(asked):
        core = cores[j * size : (j + 1) * size]
        mixed = dot_nn(core, hidden[:, j * each : (j + 1) * each]).astype(BF)
        hold[j] = dot_tn(mixed, basis[...]).astype(BF)
        copies.append(
            pltpu.make_async_copy(hold.at[j], out.at[pl.ds(j * each, each)], sent.at[j])
        )
        copies[j].start()
    for copy in copies:
        copy.wait()


def around_y(value, d):
    size = lax.axis_size("feature")
    return lax.ppermute(value, "feature", [(i, (i + d * CORES) % size) for i in range(size)])


def other_core(value):
    size = lax.axis_size("feature")
    return lax.ppermute(value, "feature", [(i, i ^ 1) for i in range(size)])


def over_feature(value, gram_size):
    rows, lanes = value.shape
    pair = call(pair_body, shape((rows, lanes + gram_size), BF), value, other_core(value))
    return [pair] + [around_y(pair, d) for d in (1, 3, 2)]


def on_device(adapter_down, adapter_up, fisher, init_v, init_u, prompt_rows, request_ids):
    ways = lax.axis_size("adapter")
    width = adapter_down.shape[-1]
    size = init_v.shape[1]
    down = adapter_down.reshape(-1, width)
    up = adapter_up.reshape(-1, width)
    count = down.shape[0]
    rows = prompt_rows.shape[0]
    blocks = request_ids.shape[0]
    position = lax.axis_index("adapter")
    fisher_row = jnp.repeat(fisher, RANK)[None, :]
    tile = (size * width // ways // 128, 128)
    tile_shape = shape((ways, *tile), BF)
    flat = shape((size, count), F32)
    digits = jnp.stack([request_ids // RANK, request_ids % RANK]).astype(BF)
    id_tile = lax.dynamic_update_slice(jnp.zeros(tile, BF), digits, (0, position * blocks))

    def swap(parts):
        return lax.all_to_all(parts, "adapter", 0, 0, tiled=True)

    def reduced(tiles):
        return swap(call(sum_body, tile_shape, swap(tiles)))

    def projected(numer, stack):
        value = call(project_body, shape((size, count + size), F32), numer, stack)
        return over_feature(value, size)

    value = call(
        start_body,
        shape((size, 2 * count), F32),
        down,
        up,
        init_v.T.astype(BF),
        init_u.T.astype(BF),
    )
    parts, id_tile = lax.optimization_barrier((over_feature(value, 0), id_tile))
    tiles, q, p = call(first_body, [tile_shape, flat, flat], *parts, up, fisher_row)
    for sweep in range(SWEEPS):
        if sweep == 0:
            copies = call(
                sum_ids_body, shape((ways, 2 * tile[0], 128), BF), swap(tiles), id_tile
            )
            value, every_id = call(
                project_ids_body,
                [shape((size, count + size), F32), shape((1, 128), jnp.int32)],
                swap(copies),
                up,
            )
            local_id = every_id[0, : ways * blocks] - position * fisher.shape[0]
            parts, pick_rows = lax.optimization_barrier(
                (over_feature(value, size), jnp.repeat(local_id, RANK)[:, None])
            )
        else:
            numer = reduced(tiles)
            parts = projected(numer, up)
        if sweep < SWEEPS - 1:
            tiles, q = call(renew_body, [tile_shape, flat], *parts, p, down, fisher_row)
            parts = projected(reduced(tiles), down)
            tiles, p = call(renew_body, [tile_shape, flat], *parts, q, up, fisher_row)
        else:
            tiles, q, basis = call(
                last_renew_body,
                [tile_shape, flat, shape((size, width), BF)],
                *parts,
                p,
                down,
                fisher_row,
                numer,
            )
    core = jnp.full((1,), lax.axis_index("feature") % CORES, jnp.int32)
    packed = blocks * RANK * 3 // 4
    picked, hidden, gram = call(
        pick_body,
        [shape((ways, packed, 2 * size), BF), shape((size, rows), F32), shape((size, size), F32)],
        core,
        reduced(tiles),
        down,
        prompt_rows,
        q,
        pick_rows,
    )
    value = call(
        join_body, shape((size, rows + 3 * size), F32), core, swap(picked), hidden, gram
    )
    whole = pl.BlockSpec(memory_space=pltpu.VMEM)
    parts = over_feature(value, size)
    return pl.pallas_call(
        serve_body,
        out_shape=shape((rows, width), BF),
        in_specs=[whole] * (len(parts) + 1),
        out_specs=pl.BlockSpec(memory_space=pl.ANY),
        scratch_shapes=[
            pltpu.VMEM((blocks, rows // blocks, width), BF),
            pltpu.SemaphoreType.DMA((blocks,)),
        ],
        compiler_params=pltpu.CompilerParams(vmem_limit_bytes=40 * 1024 * 1024),
    )(*parts, basis)


def solution(mesh):
    placed = (
        P("adapter", None, "feature"),
        P("adapter", None, "feature"),
        P("adapter"),
        P("feature", None),
        P("feature", None),
        P("adapter", "feature"),
        P("adapter"),
    )
    return jax.shard_map(
        on_device, mesh=mesh, in_specs=placed, out_specs=P("adapter", "feature"), check_vma=False
    )
```

```python
import jax
import jax.numpy as jnp
from jax import lax
from jax.experimental import pallas as pl
from jax.experimental.pallas import tpu as pltpu
from jax.sharding import PartitionSpec as P

SWEEPS = 3
RANK = 16
CORES = 2
BF = jnp.bfloat16
F32 = jnp.float32


def call(body, outs, *args):
    whole = pl.BlockSpec(memory_space=pltpu.VMEM)
    scalar = pl.BlockSpec(memory_space=pltpu.SMEM)
    single = not isinstance(outs, (list, tuple))
    return pl.pallas_call(
        body,
        out_shape=outs,
        in_specs=[scalar if arg.shape == (1,) else whole for arg in args],
        out_specs=whole if single else [whole] * len(outs),
        compiler_params=pltpu.CompilerParams(vmem_limit_bytes=40 * 1024 * 1024),
    )(*args)


def shape(dims, dtype):
    return jax.ShapeDtypeStruct(dims, dtype)


def dot_nt(a, b, precision=None):
    return lax.dot_general(
        a, b, (((1,), (1,)), ((), ())), preferred_element_type=F32, precision=precision
    )


def dot_tn(a, b, precision=None):
    return lax.dot_general(
        a, b, (((0,), (0,)), ((), ())), preferred_element_type=F32, precision=precision
    )


def dot_nn(a, b, precision=None):
    return jnp.dot(a, b, preferred_element_type=F32, precision=precision)


def in_three(product, a, b):
    a_high, b_high = a.astype(BF), b.astype(BF)
    a_low = (a - a_high.astype(F32)).astype(BF)
    b_low = (b - b_high.astype(F32)).astype(BF)
    return product(a_high, b_high) + (product(a_high, b_low) + product(a_low, b_high))


def inverse_factor(gram):
    size = gram.shape[0]
    rows = lax.broadcasted_iota(jnp.int32, (size, size), 0)
    lanes = lax.broadcasted_iota(jnp.int32, (size, size), 1)
    eye = rows == lanes
    diagonal = jnp.where(eye, gram, 0.0)
    by_row = lax.rsqrt(jnp.sum(diagonal, axis=1, keepdims=True))
    by_lane = lax.rsqrt(jnp.sum(diagonal, axis=0, keepdims=True))
    work = jnp.concatenate([gram * by_row * by_lane, eye.astype(F32)], axis=1)
    group = 8
    whole = (group, 2 * size)
    blocks = [work[group * i : group * (i + 1)] for i in range(size // group)]
    within = lax.broadcasted_iota(jnp.int32, whole, 0)
    for b in range(len(blocks)):
        first = group * b
        columns = [
            {
                j: jnp.broadcast_to(blocks[j][:, first + m : first + m + 1], whole)
                for j in range(b, len(blocks))
            }
            for m in range(group)
        ]
        pivot_rows = [blocks[b][i : i + 1] for i in range(group)]
        pivots = {
            (i, m): columns[m][b][i : i + 1] for i in range(group) for m in range(i, group)
        }
        solved = []
        for p in range(0, group, 2):
            top, mix, low = pivots[p, p], pivots[p, p + 1], pivots[p + 1, p + 1]
            over = 1.0 / (top * low - mix * mix)
            a, b01, c = low * over, -mix * over, top * over
            factors = []
            for i in range(p + 2, group):
                x, y = pivots[p, i], pivots[p + 1, i]
                factors.append((i, a * x + b01 * y, b01 * x + c * y))
            for i, u, v in factors:
                for m in range(i, group):
                    pivots[i, m] = pivots[i, m] - (u * pivots[p, m] + v * pivots[p + 1, m])
                pivot_rows[i] = pivot_rows[i] - (u * pivot_rows[p] + v * pivot_rows[p + 1])
            solved.append((a, b01, c, factors))
        terms = [None] * group
        for p in range(group - 2, -1, -2):
            a, b01, c, factors = solved[p // 2]
            t0 = a * pivot_rows[p] + b01 * pivot_rows[p + 1]
            t1 = b01 * pivot_rows[p] + c * pivot_rows[p + 1]
            for i, u, v in factors:
                t0 = t0 - u * terms[i]
                t1 = t1 - v * terms[i]
            terms[p], terms[p + 1] = t0, t1
        for j in range(b + 1, len(blocks)):
            for m in range(group):
                blocks[j] = blocks[j] - columns[m][j] * terms[m]
        done = blocks[b]
        for p in range(0, group, 2):
            second = pivot_rows[p + 1] - (pivots[p, p + 1] / pivots[p, p]) * pivot_rows[p]
            done = jnp.where(within == p, pivot_rows[p], done)
            done = jnp.where(within == p + 1, second, done)
        blocks[b] = done
    work = jnp.concatenate(blocks, axis=0)
    diagonal = jnp.sum(jnp.where(eye, work[:, :size], 0.0), axis=1, keepdims=True)
    return work[:, size:] * lax.rsqrt(diagonal) * by_lane


def write_copies(ref, value):
    for i in range(ref.shape[0]):
        ref[i] = value


def halves(gram):
    high = gram.astype(BF)
    low = (gram - high.astype(F32)).astype(BF)
    return jnp.concatenate([high, low], axis=1)


def weighted_terms(fresh, other, fisher_row):
    count = fresh.shape[1]
    inner = in_three(dot_tn, fresh, fresh)
    a = lax.broadcasted_iota(jnp.int32, (count, count), 0) // RANK
    b = lax.broadcasted_iota(jnp.int32, (count, count), 1) // RANK
    inner = jnp.where(a == b, inner, 0.0)
    return (in_three(dot_nn, other, inner) * fisher_row).astype(BF)


def added(refs):
    total = refs[0][...].astype(F32)
    for ref in refs[1:]:
        total = total + ref[...].astype(F32)
    return total


def write_tiles(ref, value):
    across = value.shape[1] // 128
    for i in range(ref.shape[0]):
        r, c = divmod(i, across)
        ref[i] = value[16 * r : 16 * r + 16, 128 * c : 128 * c + 128].astype(BF)


def read_tiles(ref, width):
    across = width // 128
    down = ref.shape[0] // across
    return jnp.concatenate(
        [
            jnp.concatenate([ref[r * across + c, :16] for c in range(across)], axis=1)
            for r in range(down)
        ],
        axis=0,
    )


def start_body(down, up, vt, ut, out):
    q = dot_nt(ut[...], up[...])
    p = dot_nt(vt[...], down[...])
    out[...] = jnp.concatenate([q, p], axis=1)


def pair_body(own, got, out):
    total = own[...] + got[...]
    plain = 2 * total.shape[1] - out.shape[1]
    if plain == total.shape[1]:
        out[...] = total.astype(BF)
    else:
        out[...] = jnp.concatenate([total[:, :plain].astype(BF), halves(total[:, plain:])], axis=1)


def first_body(a, b, c, d, stack, fisher_row, tiles, q_out, p_out):
    total = added((a, b, c, d))
    count = total.shape[1] // 2
    q, p = total[:, :count], total[:, count:]
    q_out[...] = q
    p_out[...] = p
    terms = weighted_terms(p, q, fisher_row[...])
    write_tiles(tiles, dot_nn(terms, stack[...]))


def summed(ref):
    total = ref[0].astype(F32)
    for i in range(1, ref.shape[0]):
        total = total + ref[i].astype(F32)
    return total


def sum_body(parts, out):
    write_copies(out, summed(parts).astype(BF))


def sum_ids_body(parts, ids, out):
    write_copies(out, jnp.concatenate([summed(parts).astype(BF), ids[...]], axis=0))


def project_body(tiles, stack, out):
    numer = read_tiles(tiles, stack.shape[1])
    out[...] = jnp.concatenate([dot_nt(numer, stack[...]), dot_nt(numer, numer)], axis=1)


def keep_body(value, out):
    out[...] = value[...]


def project_ids_body(tiles, stack, out, ids_out):
    project_body(tiles, stack, out)
    ids = summed(tiles.at[:, 16:])
    ids_out[...] = (ids[0:1] * RANK + ids[1:2]).astype(jnp.int32)


def split_gram(total, at, size):
    return total[:, at : at + size] + total[:, at + size : at + 2 * size]


def renew(parts, other, stack, fisher_row, tiles, fresh_out):
    total = added(parts)
    size, count = other.shape
    inverse = inverse_factor(split_gram(total, count, size))
    fresh = in_three(dot_nn, inverse, total[:, :count])
    fresh_out[...] = fresh
    terms = weighted_terms(fresh, other[...], fisher_row[...])
    write_tiles(tiles, dot_nn(terms, stack[...]))
    return inverse


def renew_body(a, b, c, d, other, stack, fisher_row, tiles, fresh_out):
    renew((a, b, c, d), other, stack, fisher_row, tiles, fresh_out)


def last_renew_body(
    a, b, c, d, other, stack, fisher_row, numer_tiles, tiles, fresh_out, basis_out
):
    inverse = renew((a, b, c, d), other, stack, fisher_row, tiles, fresh_out)
    numer = read_tiles(numer_tiles, stack.shape[1]).astype(F32)
    basis_out[...] = in_three(dot_nn, inverse, numer).astype(BF)


def side_by_side(value):
    half = value.shape[0] // 2
    lanes = lax.broadcasted_iota(jnp.int32, (half, value.shape[1]), 1)
    return jnp.where(lanes < value.shape[1] // 2, value[:half], value[half:])


def one_below_other(value):
    half = value.shape[1] // 2
    return jnp.concatenate([value[:, :half], value[:, half:]], axis=0)


def pick_body(core, tiles, stack, prompts, q_ref, ids, picked, hidden_out, gram_out):
    numer = read_tiles(tiles, stack.shape[1])
    z = dot_nt(stack[...], numer).astype(BF)
    q = q_ref[...].T.astype(BF)
    count, size = z.shape
    ways = picked.shape[0]
    wanted = ids.shape[0]
    r = lax.broadcasted_iota(jnp.int32, (wanted, count), 0)
    c = lax.broadcasted_iota(jnp.int32, (wanted, count), 1)
    hot = (ids[...] * RANK + (r & (RANK - 1)) == c).astype(F32).astype(BF)
    chosen = dot_nn(hot, jnp.concatenate([z, z, q, q], axis=1))
    chosen_z, chosen_q = chosen[:, : 2 * size], chosen[:, 2 * size :]
    each = wanted // ways
    for i in range(ways):
        at = i * each
        first = chosen_q[at : at + each // 2]
        second = chosen_q[at + each // 2 : at + each]
        mine = jnp.where(core[0] == 0, first, second)
        picked[i] = jnp.concatenate(
            [side_by_side(chosen_z[at : at + each]), side_by_side(mine)], axis=0
        ).astype(BF)
    hidden_out[...] = dot_nt(numer, prompts[...])
    gram_out[...] = dot_nt(numer, numer)


def join_body(core, parts, hidden, gram, out):
    total = summed(parts)
    size = gram.shape[1]
    cut = total.shape[0] * 2 // 3
    z = one_below_other(total[:cut])
    q = one_below_other(total[cut:])
    none = jnp.zeros_like(q)
    q = jnp.where(
        core[0] == 0, jnp.concatenate([q, none], axis=0), jnp.concatenate([none, q], axis=0)
    )
    out[...] = jnp.concatenate([hidden[...], z, q, gram[...]], axis=1)


def serve_body(a, b, c, d, basis, out, hold, sent):
    total = added((a, b, c, d))
    size = total.shape[0]
    rows = out.shape[0]
    asked = size // RANK
    each = rows // asked
    z = total[:, rows : rows + size]
    q = a[:, rows + size : rows + 2 * size]
    z_high = z.astype(BF)
    z_low = (z - z_high.astype(F32)).astype(BF)
    crossed = []
    for j in range(asked):
        take = slice(j * RANK, (j + 1) * RANK)
        crossed.append(dot_tn(q[take], z_high[take]) + dot_tn(q[take], z_low[take]))
    inverse = inverse_factor(split_gram(total, rows + 2 * size, size))
    cores = in_three(dot_nt, jnp.concatenate(crossed, axis=0), inverse).astype(BF)
    hidden = in_three(dot_nn, inverse, total[:, :rows]).astype(BF)
    copies = []
    for j in range(asked):
        core = cores[j * size : (j + 1) * size]
        mixed = dot_nn(core, hidden[:, j * each : (j + 1) * each]).astype(BF)
        hold[j] = dot_tn(mixed, basis[...]).astype(BF)
        copies.append(
            pltpu.make_async_copy(hold.at[j], out.at[pl.ds(j * each, each)], sent.at[j])
        )
        copies[j].start()
    for copy in copies:
        copy.wait()


def around_y(value, d):
    size = lax.axis_size("feature")
    return lax.ppermute(value, "feature", [(i, (i + d * CORES) % size) for i in range(size)])


def other_core(value):
    size = lax.axis_size("feature")
    return lax.ppermute(value, "feature", [(i, i ^ 1) for i in range(size)])


def over_feature(value, gram_size):
    rows, lanes = value.shape
    pair = call(pair_body, shape((rows, lanes + gram_size), BF), value, other_core(value))
    return [pair] + [around_y(pair, d) for d in (2, 3, 1)]


def on_device(adapter_down, adapter_up, fisher, init_v, init_u, prompt_rows, request_ids):
    ways = lax.axis_size("adapter")
    width = adapter_down.shape[-1]
    size = init_v.shape[1]
    down = adapter_down.reshape(-1, width)
    up = adapter_up.reshape(-1, width)
    count = down.shape[0]
    rows = prompt_rows.shape[0]
    blocks = request_ids.shape[0]
    position = lax.axis_index("adapter")
    fisher_row = jnp.repeat(fisher, RANK)[None, :]
    tile = (size * width // ways // 128, 128)
    tile_shape = shape((ways, *tile), BF)
    flat = shape((size, count), F32)
    digits = jnp.stack([request_ids // RANK, request_ids % RANK]).astype(BF)
    id_tile = lax.dynamic_update_slice(jnp.zeros(tile, BF), digits, (0, position * blocks))

    def swap(parts):
        return lax.all_to_all(parts, "adapter", 0, 0, tiled=True)

    def reduced(tiles):
        return swap(call(sum_body, tile_shape, swap(tiles)))

    def projected(numer, stack):
        value = call(project_body, shape((size, count + size), F32), numer, stack)
        return over_feature(value, size)

    value = call(
        start_body,
        shape((size, 2 * count), F32),
        down,
        up,
        init_v.T.astype(BF),
        init_u.T.astype(BF),
    )
    core = jnp.full((1,), lax.axis_index("feature") % CORES, jnp.int32)
    parts, id_tile, core = lax.optimization_barrier((over_feature(value, 0), id_tile, core))
    tiles, q, p = call(first_body, [tile_shape, flat, flat], *parts, up, fisher_row)
    for sweep in range(SWEEPS):
        if sweep == 0:
            copies = call(
                sum_ids_body, shape((ways, 2 * tile[0], 128), BF), swap(tiles), id_tile
            )
            value, every_id = call(
                project_ids_body,
                [shape((size, count + size), F32), shape((1, 128), jnp.int32)],
                swap(copies),
                up,
            )
            local_id = every_id[0, : ways * blocks] - position * fisher.shape[0]
            pick_rows = jnp.repeat(local_id, RANK)[:, None]
            pick_rows = call(keep_body, shape(pick_rows.shape, jnp.int32), pick_rows)
            parts, pick_rows = lax.optimization_barrier((over_feature(value, size), pick_rows))
        else:
            numer = reduced(tiles)
            parts = projected(numer, up)
        if sweep < SWEEPS - 1:
            tiles, q = call(renew_body, [tile_shape, flat], *parts, p, down, fisher_row)
            parts = projected(reduced(tiles), down)
            tiles, p = call(renew_body, [tile_shape, flat], *parts, q, up, fisher_row)
        else:
            tiles, q, basis = call(
                last_renew_body,
                [tile_shape, flat, shape((size, width), BF)],
                *parts,
                p,
                down,
                fisher_row,
                numer,
            )
    packed = blocks * RANK * 3 // 4
    picked, hidden, gram = call(
        pick_body,
        [shape((ways, packed, 2 * size), BF), shape((size, rows), F32), shape((size, size), F32)],
        core,
        reduced(tiles),
        down,
        prompt_rows,
        q,
        pick_rows,
    )
    value = call(
        join_body, shape((size, rows + 3 * size), F32), core, swap(picked), hidden, gram
    )
    whole = pl.BlockSpec(memory_space=pltpu.VMEM)
    parts = over_feature(value, size)
    return pl.pallas_call(
        serve_body,
        out_shape=shape((rows, width), BF),
        in_specs=[whole] * (len(parts) + 1),
        out_specs=pl.BlockSpec(memory_space=pl.ANY),
        scratch_shapes=[
            pltpu.VMEM((blocks, rows // blocks, width), BF),
            pltpu.SemaphoreType.DMA((blocks,)),
        ],
        compiler_params=pltpu.CompilerParams(vmem_limit_bytes=40 * 1024 * 1024),
    )(*parts, basis)


def solution(mesh):
    placed = (
        P("adapter", None, "feature"),
        P("adapter", None, "feature"),
        P("adapter"),
        P("feature", None),
        P("feature", None),
        P("adapter", "feature"),
        P("adapter"),
    )
    return jax.shard_map(
        on_device, mesh=mesh, in_specs=placed, out_specs=P("adapter", "feature"), check_vma=False
    )
```

```python
import jax
import jax.numpy as jnp
from jax import lax
from jax.experimental import pallas as pl
from jax.experimental.pallas import tpu as pltpu
from jax.sharding import PartitionSpec as P

SWEEPS = 3
RANK = 16
CORES = 2
BF = jnp.bfloat16
F32 = jnp.float32


def call(body, outs, *args):
    whole = pl.BlockSpec(memory_space=pltpu.VMEM)
    scalar = pl.BlockSpec(memory_space=pltpu.SMEM)
    single = not isinstance(outs, (list, tuple))
    return pl.pallas_call(
        body,
        out_shape=outs,
        in_specs=[scalar if arg.shape == (1,) else whole for arg in args],
        out_specs=whole if single else [whole] * len(outs),
        compiler_params=pltpu.CompilerParams(vmem_limit_bytes=40 * 1024 * 1024),
    )(*args)


def shape(dims, dtype):
    return jax.ShapeDtypeStruct(dims, dtype)


def dot_nt(a, b, precision=None):
    return lax.dot_general(
        a, b, (((1,), (1,)), ((), ())), preferred_element_type=F32, precision=precision
    )


def dot_tn(a, b, precision=None):
    return lax.dot_general(
        a, b, (((0,), (0,)), ((), ())), preferred_element_type=F32, precision=precision
    )


def dot_nn(a, b, precision=None):
    return jnp.dot(a, b, preferred_element_type=F32, precision=precision)


def in_three(product, a, b):
    a_high, b_high = a.astype(BF), b.astype(BF)
    a_low = (a - a_high.astype(F32)).astype(BF)
    b_low = (b - b_high.astype(F32)).astype(BF)
    return product(a_high, b_high) + (product(a_high, b_low) + product(a_low, b_high))


def inverse_factor(gram):
    size = gram.shape[0]
    rows = lax.broadcasted_iota(jnp.int32, (size, size), 0)
    lanes = lax.broadcasted_iota(jnp.int32, (size, size), 1)
    eye = rows == lanes
    diagonal = jnp.where(eye, gram, 0.0)
    by_row = lax.rsqrt(jnp.sum(diagonal, axis=1, keepdims=True))
    by_lane = lax.rsqrt(jnp.sum(diagonal, axis=0, keepdims=True))
    work = jnp.concatenate([gram * by_row * by_lane, eye.astype(F32)], axis=1)
    group = 8
    whole = (group, 2 * size)
    blocks = [work[group * i : group * (i + 1)] for i in range(size // group)]
    within = lax.broadcasted_iota(jnp.int32, whole, 0)
    for b in range(len(blocks)):
        first = group * b
        columns = [
            {
                j: jnp.broadcast_to(blocks[j][:, first + m : first + m + 1], whole)
                for j in range(b, len(blocks))
            }
            for m in range(group)
        ]
        pivot_rows = [blocks[b][i : i + 1] for i in range(group)]
        pivots = {
            (i, m): columns[m][b][i : i + 1] for i in range(group) for m in range(i, group)
        }
        solved = []
        for p in range(0, group, 2):
            top, mix, low = pivots[p, p], pivots[p, p + 1], pivots[p + 1, p + 1]
            over = 1.0 / (top * low - mix * mix)
            a, b01, c = low * over, -mix * over, top * over
            factors = []
            for i in range(p + 2, group):
                x, y = pivots[p, i], pivots[p + 1, i]
                factors.append((i, a * x + b01 * y, b01 * x + c * y))
            for i, u, v in factors:
                for m in range(i, group):
                    pivots[i, m] = pivots[i, m] - (u * pivots[p, m] + v * pivots[p + 1, m])
                pivot_rows[i] = pivot_rows[i] - (u * pivot_rows[p] + v * pivot_rows[p + 1])
            solved.append((a, b01, c, factors))
        terms = [None] * group
        for p in range(group - 2, -1, -2):
            a, b01, c, factors = solved[p // 2]
            t0 = a * pivot_rows[p] + b01 * pivot_rows[p + 1]
            t1 = b01 * pivot_rows[p] + c * pivot_rows[p + 1]
            for i, u, v in factors:
                t0 = t0 - u * terms[i]
                t1 = t1 - v * terms[i]
            terms[p], terms[p + 1] = t0, t1
        for j in range(b + 1, len(blocks)):
            for m in range(group):
                blocks[j] = blocks[j] - columns[m][j] * terms[m]
        done = blocks[b]
        for p in range(0, group, 2):
            second = pivot_rows[p + 1] - (pivots[p, p + 1] / pivots[p, p]) * pivot_rows[p]
            done = jnp.where(within == p, pivot_rows[p], done)
            done = jnp.where(within == p + 1, second, done)
        blocks[b] = done
    work = jnp.concatenate(blocks, axis=0)
    diagonal = jnp.sum(jnp.where(eye, work[:, :size], 0.0), axis=1, keepdims=True)
    return work[:, size:] * lax.rsqrt(diagonal) * by_lane


def write_copies(ref, value):
    for i in range(ref.shape[0]):
        ref[i] = value


def halves(gram):
    high = gram.astype(BF)
    low = (gram - high.astype(F32)).astype(BF)
    return jnp.concatenate([high, low], axis=1)


def weighted_terms(fresh, other, fisher_row):
    count = fresh.shape[1]
    inner = in_three(dot_tn, fresh, fresh)
    a = lax.broadcasted_iota(jnp.int32, (count, count), 0) // RANK
    b = lax.broadcasted_iota(jnp.int32, (count, count), 1) // RANK
    inner = jnp.where(a == b, inner, 0.0)
    return (in_three(dot_nn, other, inner) * fisher_row).astype(BF)


def added(refs):
    total = refs[0][...].astype(F32)
    for ref in refs[1:]:
        total = total + ref[...].astype(F32)
    return total


def write_tiles(ref, value):
    across = value.shape[1] // 128
    for i in range(ref.shape[0]):
        r, c = divmod(i, across)
        ref[i] = value[16 * r : 16 * r + 16, 128 * c : 128 * c + 128].astype(BF)


def read_tiles(ref, width):
    across = width // 128
    down = ref.shape[0] // across
    return jnp.concatenate(
        [
            jnp.concatenate([ref[r * across + c, :16] for c in range(across)], axis=1)
            for r in range(down)
        ],
        axis=0,
    )


def start_body(down, up, vt, ut, out):
    q = dot_nt(ut[...], up[...])
    p = dot_nt(vt[...], down[...])
    out[...] = jnp.concatenate([q, p], axis=1)


def pair_body(own, got, out):
    total = own[...] + got[...]
    plain = 2 * total.shape[1] - out.shape[1]
    if plain == total.shape[1]:
        out[...] = total.astype(BF)
    else:
        out[...] = jnp.concatenate([total[:, :plain].astype(BF), halves(total[:, plain:])], axis=1)


def first_body(a, b, c, d, stack, fisher_row, tiles, p_out):
    total = added((a, b, c, d))
    count = total.shape[1] // 2
    q, p = total[:, :count], total[:, count:]
    p_out[...] = p
    terms = weighted_terms(p, q, fisher_row[...])
    write_tiles(tiles, dot_nn(terms, stack[...]))


def summed(ref):
    total = ref[0].astype(F32)
    for i in range(1, ref.shape[0]):
        total = total + ref[i].astype(F32)
    return total


def sum_body(parts, out):
    write_copies(out, summed(parts).astype(BF))


def sum_ids_body(parts, ids, out):
    write_copies(out, jnp.concatenate([summed(parts).astype(BF), ids[...]], axis=0))


def project_body(tiles, stack, out):
    numer = read_tiles(tiles, stack.shape[1])
    out[...] = jnp.concatenate([dot_nt(numer, stack[...]), dot_nt(numer, numer)], axis=1)


def keep_body(value, out):
    out[...] = value[...]


def project_ids_body(tiles, stack, out, ids_out):
    project_body(tiles, stack, out)
    ids = summed(tiles.at[:, 16:])
    ids_out[...] = (ids[0:1] * RANK + ids[1:2]).astype(jnp.int32)


def split_gram(total, at, size):
    return total[:, at : at + size] + total[:, at + size : at + 2 * size]


def renew(parts, other, stack, fisher_row, tiles, fresh_out):
    total = added(parts)
    size, count = other.shape
    inverse = inverse_factor(split_gram(total, count, size))
    fresh = in_three(dot_nn, inverse, total[:, :count])
    fresh_out[...] = fresh
    terms = weighted_terms(fresh, other[...], fisher_row[...])
    write_tiles(tiles, dot_nn(terms, stack[...]))
    return inverse


def renew_body(a, b, c, d, other, stack, fisher_row, tiles, fresh_out):
    renew((a, b, c, d), other, stack, fisher_row, tiles, fresh_out)


def last_renew_body(
    a, b, c, d, other, stack, fisher_row, numer_tiles, tiles, fresh_out, basis_out
):
    inverse = renew((a, b, c, d), other, stack, fisher_row, tiles, fresh_out)
    numer = read_tiles(numer_tiles, stack.shape[1]).astype(F32)
    basis_out[...] = in_three(dot_nn, inverse, numer).astype(BF)


def side_by_side(value):
    half = value.shape[0] // 2
    lanes = lax.broadcasted_iota(jnp.int32, (half, value.shape[1]), 1)
    return jnp.where(lanes < value.shape[1] // 2, value[:half], value[half:])


def one_below_other(value):
    half = value.shape[1] // 2
    return jnp.concatenate([value[:, :half], value[:, half:]], axis=0)


def pick_body(core, tiles, stack, prompts, q_ref, ids, picked, hidden_out, gram_out):
    numer = read_tiles(tiles, stack.shape[1])
    z = dot_nt(stack[...], numer).astype(BF)
    q = q_ref[...].T.astype(BF)
    count, size = z.shape
    ways = picked.shape[0]
    wanted = ids.shape[0]
    r = lax.broadcasted_iota(jnp.int32, (wanted, count), 0)
    c = lax.broadcasted_iota(jnp.int32, (wanted, count), 1)
    hot = (ids[...] * RANK + (r & (RANK - 1)) == c).astype(F32).astype(BF)
    chosen = dot_nn(hot, jnp.concatenate([z, z, q, q], axis=1))
    chosen_z, chosen_q = chosen[:, : 2 * size], chosen[:, 2 * size :]
    each = wanted // ways
    for i in range(ways):
        at = i * each
        first = chosen_q[at : at + each // 2]
        second = chosen_q[at + each // 2 : at + each]
        mine = jnp.where(core[0] == 0, first, second)
        picked[i] = jnp.concatenate(
            [side_by_side(chosen_z[at : at + each]), side_by_side(mine)], axis=0
        ).astype(BF)
    hidden_out[...] = dot_nt(numer, prompts[...])
    gram_out[...] = dot_nt(numer, numer)


def join_body(core, parts, hidden, gram, out):
    total = summed(parts)
    size = gram.shape[1]
    cut = total.shape[0] * 2 // 3
    z = one_below_other(total[:cut])
    q = one_below_other(total[cut:])
    none = jnp.zeros_like(q)
    q = jnp.where(
        core[0] == 0, jnp.concatenate([q, none], axis=0), jnp.concatenate([none, q], axis=0)
    )
    out[...] = jnp.concatenate([hidden[...], z, q, gram[...]], axis=1)


def serve_body(a, b, c, d, basis, out, hold, sent):
    total = added((a, b, c, d))
    size = total.shape[0]
    rows = out.shape[0]
    asked = size // RANK
    each = rows // asked
    z = total[:, rows : rows + size]
    q = a[:, rows + size : rows + 2 * size]
    z_high = z.astype(BF)
    z_low = (z - z_high.astype(F32)).astype(BF)
    crossed = []
    for j in range(asked):
        take = slice(j * RANK, (j + 1) * RANK)
        crossed.append(dot_tn(q[take], z_high[take]) + dot_tn(q[take], z_low[take]))
    inverse = inverse_factor(split_gram(total, rows + 2 * size, size))
    cores = in_three(dot_nt, jnp.concatenate(crossed, axis=0), inverse).astype(BF)
    hidden = in_three(dot_nn, inverse, total[:, :rows]).astype(BF)
    copies = []
    for j in range(asked):
        core = cores[j * size : (j + 1) * size]
        mixed = dot_nn(core, hidden[:, j * each : (j + 1) * each]).astype(BF)
        hold[j] = dot_tn(mixed, basis[...]).astype(BF)
        copies.append(
            pltpu.make_async_copy(hold.at[j], out.at[pl.ds(j * each, each)], sent.at[j])
        )
        copies[j].start()
    for copy in copies:
        copy.wait()


def around_y(value, d):
    size = lax.axis_size("feature")
    return lax.ppermute(value, "feature", [(i, (i + d * CORES) % size) for i in range(size)])


def other_core(value):
    size = lax.axis_size("feature")
    return lax.ppermute(value, "feature", [(i, i ^ 1) for i in range(size)])


def over_feature(value, gram_size, steps=(2, 3, 1)):
    rows, lanes = value.shape
    pair = call(pair_body, shape((rows, lanes + gram_size), BF), value, other_core(value))
    return [pair] + [around_y(pair, d) for d in steps]


def on_device(adapter_down, adapter_up, fisher, init_v, init_u, prompt_rows, request_ids):
    ways = lax.axis_size("adapter")
    width = adapter_down.shape[-1]
    size = init_v.shape[1]
    down = adapter_down.reshape(-1, width)
    up = adapter_up.reshape(-1, width)
    count = down.shape[0]
    rows = prompt_rows.shape[0]
    blocks = request_ids.shape[0]
    position = lax.axis_index("adapter")
    fisher_row = jnp.repeat(fisher, RANK)[None, :]
    tile = (size * width // ways // 128, 128)
    tile_shape = shape((ways, *tile), BF)
    flat = shape((size, count), F32)
    digits = jnp.stack([request_ids // RANK, request_ids % RANK]).astype(BF)
    id_tile = lax.dynamic_update_slice(jnp.zeros(tile, BF), digits, (0, position * blocks))

    def swap(parts):
        return lax.all_to_all(parts, "adapter", 0, 0, tiled=True)

    def reduced(tiles):
        return swap(call(sum_body, tile_shape, swap(tiles)))

    def projected(numer, stack, steps=(2, 3, 1)):
        value = call(project_body, shape((size, count + size), F32), numer, stack)
        return over_feature(value, size, steps)

    value = call(
        start_body,
        shape((size, 2 * count), F32),
        down,
        up,
        init_v.T.astype(BF),
        init_u.T.astype(BF),
    )
    core = jnp.full((1,), lax.axis_index("feature") % CORES, jnp.int32)
    parts, id_tile, core = lax.optimization_barrier((over_feature(value, 0), id_tile, core))
    tiles, p = call(first_body, [tile_shape, flat], *parts, up, fisher_row)
    for sweep in range(SWEEPS):
        if sweep == 0:
            copies = call(
                sum_ids_body, shape((ways, 2 * tile[0], 128), BF), swap(tiles), id_tile
            )
            value, every_id = call(
                project_ids_body,
                [shape((size, count + size), F32), shape((1, 128), jnp.int32)],
                swap(copies),
                up,
            )
            local_id = every_id[0, : ways * blocks] - position * fisher.shape[0]
            pick_rows = jnp.repeat(local_id, RANK)[:, None]
            pick_rows = call(keep_body, shape(pick_rows.shape, jnp.int32), pick_rows)
            parts, pick_rows = lax.optimization_barrier((over_feature(value, size), pick_rows))
        else:
            numer = reduced(tiles)
            parts = projected(numer, up)
        if sweep < SWEEPS - 1:
            tiles, q = call(renew_body, [tile_shape, flat], *parts, p, down, fisher_row)
            parts = projected(reduced(tiles), down, (1, 2, 3) if sweep == 0 else (2, 3, 1))
            tiles, p = call(renew_body, [tile_shape, flat], *parts, q, up, fisher_row)
        else:
            tiles, q, basis = call(
                last_renew_body,
                [tile_shape, flat, shape((size, width), BF)],
                *parts,
                p,
                down,
                fisher_row,
                numer,
            )
    packed = blocks * RANK * 3 // 4
    picked, hidden, gram = call(
        pick_body,
        [shape((ways, packed, 2 * size), BF), shape((size, rows), F32), shape((size, size), F32)],
        core,
        reduced(tiles),
        down,
        prompt_rows,
        q,
        pick_rows,
    )
    value = call(
        join_body, shape((size, rows + 3 * size), F32), core, swap(picked), hidden, gram
    )
    whole = pl.BlockSpec(memory_space=pltpu.VMEM)
    parts = over_feature(value, size)
    return pl.pallas_call(
        serve_body,
        out_shape=shape((rows, width), BF),
        in_specs=[whole] * (len(parts) + 1),
        out_specs=pl.BlockSpec(memory_space=pl.ANY),
        scratch_shapes=[
            pltpu.VMEM((blocks, rows // blocks, width), BF),
            pltpu.SemaphoreType.DMA((blocks,)),
        ],
        compiler_params=pltpu.CompilerParams(vmem_limit_bytes=40 * 1024 * 1024),
    )(*parts, basis)


def solution(mesh):
    placed = (
        P("adapter", None, "feature"),
        P("adapter", None, "feature"),
        P("adapter"),
        P("feature", None),
        P("feature", None),
        P("adapter", "feature"),
        P("adapter"),
    )
    return jax.shard_map(
        on_device, mesh=mesh, in_specs=placed, out_specs=P("adapter", "feature"), check_vma=False
    )
```

```python
import jax
import jax.numpy as jnp
from jax import lax
from jax.experimental import pallas as pl
from jax.experimental.pallas import tpu as pltpu
from jax.sharding import PartitionSpec as P

SWEEPS = 3
RANK = 16
CORES = 2
BF = jnp.bfloat16
F32 = jnp.float32


def call(body, outs, *args):
    whole = pl.BlockSpec(memory_space=pltpu.VMEM)
    scalar = pl.BlockSpec(memory_space=pltpu.SMEM)
    single = not isinstance(outs, (list, tuple))
    return pl.pallas_call(
        body,
        out_shape=outs,
        in_specs=[scalar if arg.shape == (1,) else whole for arg in args],
        out_specs=whole if single else [whole] * len(outs),
        compiler_params=pltpu.CompilerParams(vmem_limit_bytes=40 * 1024 * 1024),
    )(*args)


def shape(dims, dtype):
    return jax.ShapeDtypeStruct(dims, dtype)


def dot_nt(a, b, precision=None):
    return lax.dot_general(
        a, b, (((1,), (1,)), ((), ())), preferred_element_type=F32, precision=precision
    )


def dot_tn(a, b, precision=None):
    return lax.dot_general(
        a, b, (((0,), (0,)), ((), ())), preferred_element_type=F32, precision=precision
    )


def dot_nn(a, b, precision=None):
    return jnp.dot(a, b, preferred_element_type=F32, precision=precision)


def in_three(product, a, b):
    a_high, b_high = a.astype(BF), b.astype(BF)
    a_low = (a - a_high.astype(F32)).astype(BF)
    b_low = (b - b_high.astype(F32)).astype(BF)
    return product(a_high, b_high) + (product(a_high, b_low) + product(a_low, b_high))


def inverse_factor(gram):
    size = gram.shape[0]
    rows = lax.broadcasted_iota(jnp.int32, (size, size), 0)
    lanes = lax.broadcasted_iota(jnp.int32, (size, size), 1)
    eye = rows == lanes
    diagonal = jnp.where(eye, gram, 0.0)
    by_row = lax.rsqrt(jnp.sum(diagonal, axis=1, keepdims=True))
    by_lane = lax.rsqrt(jnp.sum(diagonal, axis=0, keepdims=True))
    work = jnp.concatenate([gram * by_row * by_lane, eye.astype(F32)], axis=1)
    group = 8
    whole = (group, 2 * size)
    blocks = [work[group * i : group * (i + 1)] for i in range(size // group)]
    within = lax.broadcasted_iota(jnp.int32, whole, 0)
    for b in range(len(blocks)):
        first = group * b
        columns = [
            {
                j: jnp.broadcast_to(blocks[j][:, first + m : first + m + 1], whole)
                for j in range(b, len(blocks))
            }
            for m in range(group)
        ]
        pivot_rows = [blocks[b][i : i + 1] for i in range(group)]
        pivots = {
            (i, m): columns[m][b][i : i + 1] for i in range(group) for m in range(i, group)
        }
        solved = []
        for p in range(0, group, 2):
            top, mix, low = pivots[p, p], pivots[p, p + 1], pivots[p + 1, p + 1]
            over = 1.0 / (top * low - mix * mix)
            a, b01, c = low * over, -mix * over, top * over
            factors = []
            for i in range(p + 2, group):
                x, y = pivots[p, i], pivots[p + 1, i]
                factors.append((i, a * x + b01 * y, b01 * x + c * y))
            for i, u, v in factors:
                for m in range(i, group):
                    pivots[i, m] = pivots[i, m] - (u * pivots[p, m] + v * pivots[p + 1, m])
                pivot_rows[i] = pivot_rows[i] - (u * pivot_rows[p] + v * pivot_rows[p + 1])
            solved.append((a, b01, c, factors))
        terms = [None] * group
        for p in range(group - 2, -1, -2):
            a, b01, c, factors = solved[p // 2]
            t0 = a * pivot_rows[p] + b01 * pivot_rows[p + 1]
            t1 = b01 * pivot_rows[p] + c * pivot_rows[p + 1]
            for i, u, v in factors:
                t0 = t0 - u * terms[i]
                t1 = t1 - v * terms[i]
            terms[p], terms[p + 1] = t0, t1
        for j in range(b + 1, len(blocks)):
            for m in range(group):
                blocks[j] = blocks[j] - columns[m][j] * terms[m]
        done = blocks[b]
        for p in range(0, group, 2):
            second = pivot_rows[p + 1] - (pivots[p, p + 1] / pivots[p, p]) * pivot_rows[p]
            done = jnp.where(within == p, pivot_rows[p], done)
            done = jnp.where(within == p + 1, second, done)
        blocks[b] = done
    work = jnp.concatenate(blocks, axis=0)
    diagonal = jnp.sum(jnp.where(eye, work[:, :size], 0.0), axis=1, keepdims=True)
    return work[:, size:] * lax.rsqrt(diagonal) * by_lane


def write_copies(ref, value):
    for i in range(ref.shape[0]):
        ref[i] = value


def halves(gram):
    high = gram.astype(BF)
    low = (gram - high.astype(F32)).astype(BF)
    return jnp.concatenate([high, low], axis=1)


def weighted_terms(fresh, other, fisher_row):
    count = fresh.shape[1]
    low = fresh.astype(BF)
    inner = dot_tn(low, low)
    a = lax.broadcasted_iota(jnp.int32, (count, count), 0) // RANK
    b = lax.broadcasted_iota(jnp.int32, (count, count), 1) // RANK
    inner = jnp.where(a == b, inner, 0.0)
    return (dot_nn(other.astype(BF), inner.astype(BF)) * fisher_row).astype(BF)


def added(refs):
    total = refs[0][...].astype(F32)
    for ref in refs[1:]:
        total = total + ref[...].astype(F32)
    return total


def write_tiles(ref, value):
    across = value.shape[1] // 128
    for i in range(ref.shape[0]):
        r, c = divmod(i, across)
        ref[i] = value[16 * r : 16 * r + 16, 128 * c : 128 * c + 128].astype(BF)


def read_tiles(ref, width):
    across = width // 128
    down = ref.shape[0] // across
    return jnp.concatenate(
        [
            jnp.concatenate([ref[r * across + c, :16] for c in range(across)], axis=1)
            for r in range(down)
        ],
        axis=0,
    )


def start_body(down, up, vt, ut, out, down_here, up_here, vt_here, ut_here, came):
    pairs = ((up, up_here), (ut, ut_here), (down, down_here), (vt, vt_here))
    copies = [pltpu.make_async_copy(a, b, came.at[i]) for i, (a, b) in enumerate(pairs)]
    for copy in copies:
        copy.start()
    copies[0].wait()
    copies[1].wait()
    q = dot_nt(ut_here[...].astype(BF), up_here[...])
    copies[2].wait()
    copies[3].wait()
    p = dot_nt(vt_here[...].astype(BF), down_here[...])
    out[...] = jnp.concatenate([q, p], axis=1)


def pair_body(own, got, out):
    total = own[...] + got[...]
    plain = 2 * total.shape[1] - out.shape[1]
    if plain == total.shape[1]:
        out[...] = total.astype(BF)
    else:
        out[...] = jnp.concatenate([total[:, :plain].astype(BF), halves(total[:, plain:])], axis=1)


def first_body(a, b, c, d, stack, fisher_row, tiles, p_out):
    total = added((a, b, c, d))
    count = total.shape[1] // 2
    q, p = total[:, :count], total[:, count:]
    p_out[...] = p
    terms = weighted_terms(p, q, fisher_row[...])
    write_tiles(tiles, dot_nn(terms, stack[...]))


def summed(ref):
    total = ref[0].astype(F32)
    for i in range(1, ref.shape[0]):
        total = total + ref[i].astype(F32)
    return total


def sum_body(parts, out):
    write_copies(out, summed(parts).astype(BF))


def sum_ids_body(parts, ids, out):
    write_copies(out, jnp.concatenate([summed(parts).astype(BF), ids[...]], axis=0))


def project_body(tiles, stack, out):
    numer = read_tiles(tiles, stack.shape[1])
    out[...] = jnp.concatenate([dot_nt(numer, stack[...]), dot_nt(numer, numer)], axis=1)


def keep_body(value, out):
    out[...] = value[...]


def project_ids_body(tiles, stack, out, ids_out):
    project_body(tiles, stack, out)
    ids = summed(tiles.at[:, 16:])
    ids_out[...] = (ids[0:1] * RANK + ids[1:2]).astype(jnp.int32)


def split_gram(total, at, size):
    return total[:, at : at + size] + total[:, at + size : at + 2 * size]


def renew(parts, other, stack, fisher_row, tiles, fresh_out):
    total = added(parts)
    size, count = other.shape
    inverse = inverse_factor(split_gram(total, count, size))
    fresh = in_three(dot_nn, inverse, total[:, :count])
    fresh_out[...] = fresh
    terms = weighted_terms(fresh, other[...], fisher_row[...])
    write_tiles(tiles, dot_nn(terms, stack[...]))
    return inverse


def renew_body(a, b, c, d, other, stack, fisher_row, tiles, fresh_out):
    renew((a, b, c, d), other, stack, fisher_row, tiles, fresh_out)


def last_renew_body(
    a, b, c, d, other, stack, fisher_row, numer_tiles, tiles, fresh_out, basis_out
):
    inverse = renew((a, b, c, d), other, stack, fisher_row, tiles, fresh_out)
    numer = read_tiles(numer_tiles, stack.shape[1]).astype(F32)
    basis_out[...] = in_three(dot_nn, inverse, numer).astype(BF)


def side_by_side(value):
    half = value.shape[0] // 2
    lanes = lax.broadcasted_iota(jnp.int32, (half, value.shape[1]), 1)
    return jnp.where(lanes < value.shape[1] // 2, value[:half], value[half:])


def one_below_other(value):
    half = value.shape[1] // 2
    return jnp.concatenate([value[:, :half], value[:, half:]], axis=0)


def pick_body(core, tiles, stack, prompts, q_ref, ids, picked, hidden_out, gram_out):
    numer = read_tiles(tiles, stack.shape[1])
    z = dot_nt(stack[...], numer).astype(BF)
    q = q_ref[...].T.astype(BF)
    count, size = z.shape
    ways = picked.shape[0]
    wanted = ids.shape[0]
    r = lax.broadcasted_iota(jnp.int32, (wanted, count), 0)
    c = lax.broadcasted_iota(jnp.int32, (wanted, count), 1)
    hot = (ids[...] * RANK + (r & (RANK - 1)) == c).astype(F32).astype(BF)
    chosen = dot_nn(hot, jnp.concatenate([z, z, q, q], axis=1))
    chosen_z, chosen_q = chosen[:, : 2 * size], chosen[:, 2 * size :]
    each = wanted // ways
    for i in range(ways):
        at = i * each
        first = chosen_q[at : at + each // 2]
        second = chosen_q[at + each // 2 : at + each]
        mine = jnp.where(core[0] == 0, first, second)
        picked[i] = jnp.concatenate(
            [side_by_side(chosen_z[at : at + each]), side_by_side(mine)], axis=0
        ).astype(BF)
    hidden_out[...] = dot_nt(numer, prompts[...])
    gram_out[...] = dot_nt(numer, numer)


def join_body(core, parts, hidden, gram, out):
    total = summed(parts)
    size = gram.shape[1]
    cut = total.shape[0] * 2 // 3
    z = one_below_other(total[:cut])
    q = one_below_other(total[cut:])
    none = jnp.zeros_like(q)
    q = jnp.where(
        core[0] == 0, jnp.concatenate([q, none], axis=0), jnp.concatenate([none, q], axis=0)
    )
    out[...] = jnp.concatenate([hidden[...], z, q, gram[...]], axis=1)


def serve_body(a, b, c, d, basis, out, hold, sent):
    total = added((a, b, c, d))
    size = total.shape[0]
    rows = out.shape[0]
    asked = size // RANK
    each = rows // asked
    z = total[:, rows : rows + size]
    q = a[:, rows + size : rows + 2 * size]
    z_high = z.astype(BF)
    z_low = (z - z_high.astype(F32)).astype(BF)
    crossed = []
    for j in range(asked):
        take = slice(j * RANK, (j + 1) * RANK)
        crossed.append(dot_tn(q[take], z_high[take]) + dot_tn(q[take], z_low[take]))
    inverse = inverse_factor(split_gram(total, rows + 2 * size, size))
    cores = in_three(dot_nt, jnp.concatenate(crossed, axis=0), inverse).astype(BF)
    hidden = in_three(dot_nn, inverse, total[:, :rows]).astype(BF)
    copies = []
    for j in range(asked):
        core = cores[j * size : (j + 1) * size]
        mixed = dot_nn(core, hidden[:, j * each : (j + 1) * each]).astype(BF)
        hold[j] = dot_tn(mixed, basis[...]).astype(BF)
        copies.append(
            pltpu.make_async_copy(hold.at[j], out.at[pl.ds(j * each, each)], sent.at[j])
        )
        copies[j].start()
    for copy in copies:
        copy.wait()


def around_y(value, d):
    size = lax.axis_size("feature")
    return lax.ppermute(value, "feature", [(i, (i + d * CORES) % size) for i in range(size)])


def other_core(value):
    size = lax.axis_size("feature")
    return lax.ppermute(value, "feature", [(i, i ^ 1) for i in range(size)])


def over_feature(value, gram_size, steps=(2, 1, 3)):
    rows, lanes = value.shape
    pair = call(pair_body, shape((rows, lanes + gram_size), BF), value, other_core(value))
    return [pair] + [around_y(pair, d) for d in steps]


def on_device(adapter_down, adapter_up, fisher, init_v, init_u, prompt_rows, request_ids):
    ways = lax.axis_size("adapter")
    width = adapter_down.shape[-1]
    size = init_v.shape[1]
    down = adapter_down.reshape(-1, width)
    up = adapter_up.reshape(-1, width)
    count = down.shape[0]
    rows = prompt_rows.shape[0]
    blocks = request_ids.shape[0]
    position = lax.axis_index("adapter")
    fisher_row = jnp.repeat(fisher, RANK)[None, :]
    tile = (size * width // ways // 128, 128)
    tile_shape = shape((ways, *tile), BF)
    flat = shape((size, count), F32)
    digits = jnp.stack([request_ids // RANK, request_ids % RANK]).astype(BF)
    id_tile = lax.dynamic_update_slice(jnp.zeros(tile, BF), digits, (0, position * blocks))

    def swap(parts):
        return lax.all_to_all(parts, "adapter", 0, 0, tiled=True)

    def reduced(tiles):
        return swap(call(sum_body, tile_shape, swap(tiles)))

    def projected(numer, stack, steps=(2, 1, 3)):
        value = call(project_body, shape((size, count + size), F32), numer, stack)
        return over_feature(value, size, steps)

    value = pl.pallas_call(
        start_body,
        out_shape=shape((size, 2 * count), F32),
        in_specs=[pl.BlockSpec(memory_space=pl.ANY)] * 4,
        out_specs=pl.BlockSpec(memory_space=pltpu.VMEM),
        scratch_shapes=[
            pltpu.VMEM((count, width), BF),
            pltpu.VMEM((count, width), BF),
            pltpu.VMEM((size, width), F32),
            pltpu.VMEM((size, width), F32),
            pltpu.SemaphoreType.DMA((4,)),
        ],
        compiler_params=pltpu.CompilerParams(vmem_limit_bytes=56295424),
    )(down, up, init_v.T, init_u.T)
    core = jnp.full((1,), lax.axis_index("feature") % CORES, jnp.int32)
    parts, id_tile, core = lax.optimization_barrier((over_feature(value, 0), id_tile, core))
    tiles, p = call(first_body, [tile_shape, flat], *parts, up, fisher_row)
    for sweep in range(SWEEPS):
        if sweep == 0:
            copies = call(
                sum_ids_body, shape((ways, 2 * tile[0], 128), BF), swap(tiles), id_tile
            )
            value, every_id = call(
                project_ids_body,
                [shape((size, count + size), F32), shape((1, 128), jnp.int32)],
                swap(copies),
                up,
            )
            local_id = every_id[0, : ways * blocks] - position * fisher.shape[0]
            pick_rows = jnp.repeat(local_id, RANK)[:, None]
            pick_rows = call(keep_body, shape(pick_rows.shape, jnp.int32), pick_rows)
            parts, pick_rows = lax.optimization_barrier((over_feature(value, size), pick_rows))
        else:
            numer = reduced(tiles)
            parts = projected(numer, up)
        if sweep < SWEEPS - 1:
            tiles, q = call(renew_body, [tile_shape, flat], *parts, p, down, fisher_row)
            parts = projected(reduced(tiles), down, (3, 2, 1) if sweep == 0 else (2, 1, 3))
            tiles, p = call(renew_body, [tile_shape, flat], *parts, q, up, fisher_row)
        else:
            tiles, q, basis = call(
                last_renew_body,
                [tile_shape, flat, shape((size, width), BF)],
                *parts,
                p,
                down,
                fisher_row,
                numer,
            )
    packed = blocks * RANK * 3 // 4
    picked, hidden, gram = call(
        pick_body,
        [shape((ways, packed, 2 * size), BF), shape((size, rows), F32), shape((size, size), F32)],
        core,
        reduced(tiles),
        down,
        prompt_rows,
        q,
        pick_rows,
    )
    value = call(
        join_body, shape((size, rows + 3 * size), F32), core, swap(picked), hidden, gram
    )
    whole = pl.BlockSpec(memory_space=pltpu.VMEM)
    parts = over_feature(value, size)
    return pl.pallas_call(
        serve_body,
        out_shape=shape((rows, width), BF),
        in_specs=[whole] * (len(parts) + 1),
        out_specs=pl.BlockSpec(memory_space=pl.ANY),
        scratch_shapes=[
            pltpu.VMEM((blocks, rows // blocks, width), BF),
            pltpu.SemaphoreType.DMA((blocks,)),
        ],
        compiler_params=pltpu.CompilerParams(vmem_limit_bytes=40 * 1024 * 1024),
    )(*parts, basis)


def solution(mesh):
    placed = (
        P("adapter", None, "feature"),
        P("adapter", None, "feature"),
        P("adapter"),
        P("feature", None),
        P("feature", None),
        P("adapter", "feature"),
        P("adapter"),
    )
    return jax.shard_map(
        on_device, mesh=mesh, in_specs=placed, out_specs=P("adapter", "feature"), check_vma=False
    )
```
